1024 devices in a mesh: pool: 8 (over y_lo, x), peer: 32 (over z, core), sub: 4 (over y_hi).
Axes of the slice: x: 4, y: 8 (y_hi: 4, y_lo: 2; y = y_hi * 2 + y_lo), z: 16, core: 2. Of those that a mesh axis runs over, the one named last changes fastest.
Arguments:
- x_a: bfloat16 [2048, 7168], P(('peer', 'sub'), 'pool'), may hold values from -6 to 6
- routes: int32 [2048, 8], P(('peer', 'sub')), may hold values from 0 to 31, all different within a row; in each aligned block of 16 rows (0 to 15, 16 to 31, ...) at most 5 rows name the same one
- route_score: float32 [2048, 8], P(('peer', 'sub')), may hold values from 0.05 to 1
- w_gate: bfloat16 [32, 7168, 2048], P('peer', 'pool', 'sub'), may hold values from -0.0625 to 0.0625
- w_up: bfloat16 [32, 7168, 2048], P('peer', 'pool', 'sub'), may hold values from -0.0625 to 0.0625
- w_down: bfloat16 [32, 2048, 7168], P('peer', 'sub', 'pool'), may hold values from -0.125 to 0.125
- queries: bfloat16 [1024, 128, 576], P(('pool', 'peer', 'sub')), may hold values from -64 to 64
- cache: bfloat16 [1024, 128, 576], P(('pool', 'peer', 'sub')), may hold values from -4 to 4
- lengths: int32 [1024], P(('pool', 'peer', 'sub')), may hold values from 1 to 128, as said below
Outputs:
- moe_out: bfloat16 [2048, 7168], P(('peer', 'sub'), 'pool')
- context: bfloat16 [1024, 128, 512], P(('pool', 'peer', 'sub'))
The draws below stay inside these ranges and needn't reach their ends.
Inputs may be any that keep to these rules, and one draw needn't show every extreme that they name: `routes`: each row names 8 different experts; within the rows of one device no expert is named more than 5 times. `lengths`: request 0 uses the whole cache.
All inputs are finite; a program needn't handle non-finite values.
Results may differ from the reference program's by a relative error of at most 0.011.
Values may be sent and summed in bfloat16 or wider, within the bound.
A program may use at most 32 MiB of HBM per device.

```python
import math
import jax
import jax.numpy as jnp
import numpy as np
from jax import lax

D = 7168
FF = 2048
HEADS = 128
KV_RANK = 512
ROPE_DIM = 64
NOPE_DIM = 128
TA = 16
LMAX = 128
EXPERTS = 32
TOPK = 8
MOST = 5
ENTRY = 576
TOKENS_A = 2048
TOKENS_B = 1024


def shared_cache(key):
    key_len, key_val = jax.random.split(key)
    drawn = jax.random.randint(key_len, (TOKENS_B,), 1, LMAX + 1).astype(jnp.int32)
    lengths = jnp.where(jnp.arange(TOKENS_B) == 0, LMAX, drawn).astype(jnp.int32)
    values = jnp.clip(jax.random.normal(key_val, (TOKENS_B, LMAX, ENTRY), jnp.float32), -4.0, 4.0)
    return (lengths, values)


def draw_lengths(key, part):
    lengths, values = shared_cache(key)
    return lengths


def draw_cache(key, part):
    lengths, values = shared_cache(key)
    return values.astype(jnp.bfloat16)


def draw_queries(key, part):
    key = jax.random.fold_in(key, 7)
    noise = jnp.clip(jax.random.normal(key, (TOKENS_B, HEADS, ENTRY), jnp.float32), -4.0, 4.0)
    return noise.astype(jnp.bfloat16)


def block_scale(stream_key, dims, cuts, least, largest):
    level = 1.0
    for dim, parts in cuts:
        steps = jax.random.uniform(jax.random.fold_in(jax.random.fold_in(stream_key, 6), dim), (parts,), jnp.float32, least / len(cuts), largest / len(cuts))
        level = level * jnp.repeat(jnp.exp(steps), dims[dim] // parts).reshape((-1,) + (1,) * (len(dims) - 1 - dim))
    return level


def deal_out(key, own, number, rows, number_of, top, bound, slope):
    ranking = jax.random.permutation(key, number_of)
    heavy_load, usual = portions_of(number_of, rows * top, bound, slope, True), portions_of(number_of, rows * top, bound, slope, False)
    places = jnp.arange(number_of)

    def named(sizes, offset_by):
        used = int((sizes > 0).sum())
        fixed = max(1, used // 4)
        moved = fixed + (places - fixed + offset_by * (used - fixed)) % max(1, number_of - fixed)
        return jnp.zeros((number_of,), jnp.int32).at[ranking[jnp.where(places < fixed, places, moved)]].set(jnp.asarray(sizes, jnp.int32))

    sizes = jnp.where(number % 4 == 0, named(heavy_load, number // 4), named(usual, number - number // 4 - 1))
    mixed = jax.random.permutation(jax.random.fold_in(own, 3), number_of)
    giver, receiver = mixed[0:number_of // 2 * 2:2], mixed[1:number_of // 2 * 2:2]
    room = jnp.minimum(sizes[giver] - 1, bound - sizes[receiver]) // 2
    room = jnp.where((giver == ranking[0]) | (receiver == ranking[0]) | (sizes[receiver] == 0), 0, jnp.maximum(room, 0))
    moved = jax.random.randint(jax.random.fold_in(own, 4), (number_of // 2,), 0, 1 << 20) % (room + 1)
    sizes = sizes.at[giver].add(-moved).at[receiver].add(moved)
    labels = jnp.searchsorted(jnp.cumsum(sizes), jnp.arange(rows * top), side="right").astype(jnp.int32)
    listing = labels.reshape(top, rows).T
    listing = listing[jax.random.permutation(jax.random.fold_in(own, 1), rows)]
    offset_by = jax.random.randint(jax.random.fold_in(own, 2), (rows, 1), 0, top)
    return jnp.take_along_axis(listing, (jnp.arange(top)[None, :] + offset_by) % top, axis=1)


def portions_of(amount, total, reach, skew, full):
    portions = [(1 << 20) // math.isqrt(rank ** skew) + 1 for rank in range(1, amount + 1)]
    largest = reach if full else min(reach, max(-(-total // amount), total * portions[0] // sum(portions)))
    least = 1 if total - largest >= amount - 1 else 0
    given, rest = [largest] + [least] * (amount - 1), total - largest - least * (amount - 1)
    while rest > 0:
        movable = [i for i in range(1, amount) if given[i] < largest] or [i for i in range(1, amount) if given[i] < reach]
        whole, budget = sum([portions[i] for i in movable]), rest
        for i in movable:
            more = min(reach - given[i], max(1, budget * portions[i] // whole), rest)
            given[i] = given[i] + more
            rest = rest - more
    return np.array(given)


def bell_draw(key, extent, spread, reach, cuts=(), kind=jnp.bfloat16):
    result = spread * jax.random.normal(key, extent, jnp.float32)
    if cuts:
        result = result * block_scale(key, extent, cuts, -0.22, 0.18)
    return jnp.clip(result, -reach, reach).astype(kind)


def setup_inputs(seed: int = 0) -> dict:
    key_of = jax.random.split(jax.random.key(seed), 10)
    x_a = bell_draw(key_of[0], (TOKENS_A, D), 1.0, 6.0, ((0, 128), (1, 8)))
    routes_keys = jax.random.split(jax.random.fold_in(key_of[1], 1), TOKENS_A // TA)
    routes_turns = jax.random.permutation(jax.random.fold_in(key_of[1], 3), TOKENS_A // TA)
    routes = jax.vmap(lambda own, number: deal_out(jax.random.fold_in(key_of[1], 2), own, number, TA, EXPERTS, TOPK, MOST, 2))(routes_keys, routes_turns).reshape((TOKENS_A, TOPK))
    route_score = jnp.clip(jnp.exp(math.log(1.0) - 2.9957323 * jax.random.uniform(key_of[2], (TOKENS_A, TOPK), jnp.float32) ** block_scale(key_of[2], (TOKENS_A, TOPK), ((0, 128),), -0.2, 0.2)), 0.05, 1.0)
    w_gate = bell_draw(key_of[3], (EXPERTS, D, FF), D ** -0.5, 0.0625, ((0, 32), (1, 8), (2, 4)))
    w_up = bell_draw(key_of[4], (EXPERTS, D, FF), D ** -0.5, 0.0625, ((0, 32), (1, 8), (2, 4)))
    w_down = bell_draw(key_of[5], (EXPERTS, FF, D), FF ** -0.5, 0.125, ((0, 32), (1, 4), (2, 8)))
    queries = draw_queries(jax.random.fold_in(key_of[9], 71), 0)
    cache = draw_cache(jax.random.fold_in(key_of[9], 71), 0)
    lengths = draw_lengths(jax.random.fold_in(key_of[9], 71), 0)
    return dict(x_a=x_a, routes=routes, route_score=route_score, w_gate=w_gate, w_up=w_up, w_down=w_down, queries=queries, cache=cache, lengths=lengths)


routed_scaling = 2.5


def expert_rows(packed):
    rows, gate_w, up_w, down_w = packed
    gate = jnp.dot(rows, gate_w, preferred_element_type=jnp.float32)
    upper = jnp.dot(rows, up_w, preferred_element_type=jnp.float32)
    hidden = (jax.nn.silu(gate) * upper).astype(jnp.bfloat16)
    return jnp.dot(hidden, down_w, preferred_element_type=jnp.float32).astype(jnp.bfloat16)


def reference(x_a, routes, route_score, w_gate, w_up, w_down, queries, cache, lengths):
    blocks = TOKENS_A // TA
    flat_ids = routes.reshape(blocks, TA * TOPK).astype(jnp.int32)
    expert_hit = (flat_ids[:, :, None] == jnp.arange(EXPERTS, dtype=jnp.int32)[None, None, :]).astype(jnp.int32)
    earlier = jnp.cumsum(expert_hit, axis=1) - expert_hit
    slot_index = jnp.sum(earlier * expert_hit, axis=2)
    target = (flat_ids * MOST + slot_index).astype(jnp.int32)
    token_local = (jnp.arange(TA * TOPK, dtype=jnp.int32) // TOPK).astype(jnp.int32)
    source_rows = x_a.reshape(blocks, TA, D)[:, token_local]
    buffer = jnp.zeros((blocks, EXPERTS * MOST, D), x_a.dtype)
    buffer = buffer.at[jnp.arange(blocks, dtype=jnp.int32)[:, None], target].set(source_rows)
    per_expert = buffer.reshape(blocks, EXPERTS, MOST, D).transpose(1, 0, 2, 3).reshape(EXPERTS, blocks * MOST, D)
    results = lax.map(expert_rows, (per_expert, w_gate, w_up, w_down))
    results = results.reshape(EXPERTS, blocks, MOST, D).transpose(1, 0, 2, 3).reshape(blocks, EXPERTS * MOST, D)
    picked = jnp.take_along_axis(results, target[:, :, None], axis=1).reshape(TOKENS_A, TOPK, D)
    weights = routed_scaling * route_score / jnp.sum(route_score, axis=1, keepdims=True)
    moe_out = jnp.sum(weights[:, :, None] * picked.astype(jnp.float32), axis=1).astype(jnp.bfloat16)

    scale = (NOPE_DIM + ROPE_DIM) ** -0.5
    scores = jnp.einsum("thc,tlc->thl", queries.astype(jnp.float32), cache.astype(jnp.float32)) * scale
    valid = jnp.arange(LMAX, dtype=jnp.int32)[None, None, :] < lengths[:, None, None]
    highest = jnp.max(jnp.where(valid, scores, -jnp.inf), axis=2, keepdims=True)
    expo = jnp.where(valid, jnp.exp(scores - highest), 0.0)
    probs = (expo / jnp.sum(expo, axis=2, keepdims=True)).astype(jnp.bfloat16)
    context = jnp.einsum("thl,tlc->thc", probs.astype(jnp.float32), cache[:, :, :KV_RANK].astype(jnp.float32))
    return moe_out, context.astype(jnp.bfloat16)
```

```python
import functools

import jax
import jax.numpy as jnp
from jax import lax
from jax.experimental import pallas as pl
from jax.experimental.pallas import tpu as pltpu
from jax.sharding import PartitionSpec as P

KV_RANK = 512
SCALE = 192 ** (-0.5)
ROUTED = 2.5
TOK = 16
MOST = 5
WIDTH = 896
WIDE = 1024
FFS = 512
GROUP = 16 * MOST
SHARE = FFS // 4
MESH = pl.DeviceIdType.MESH
F32, BF16 = jnp.float32, jnp.bfloat16


def kernel(
    x_ref, routes_ref, score_ref, len_ref, wg_hbm, wu_hbm, wd_hbm, q_hbm, c_hbm,
    moe_ref, ctx_hbm,
    xb, wg, wu, wd, qv, cv, ctxv, sp, rp, hr, co, cs, cm, zs, zr, fs, yr,
    load_sem, y_send, y_recv, ring_send, ring_recv, mate_send, mate_recv,
    rp_send, rp_recv, h_send, h_recv, cm_send, cm_recv, z_send, z_recv, f_send, f_recv,
):
    pool, peer, sub = lax.axis_index("pool"), lax.axis_index("peer"), lax.axis_index("sub")
    row, col = pool // 4, lax.rem(pool, 4)
    up_dev = {"peer": lax.rem(peer + 2, 32)}
    down_dev = {"peer": lax.rem(peer + 30, 32)}
    mate_dev = {"peer": peer + 1 - 2 * lax.rem(peer, 2)}

    def sub_dev(d):
        return {"sub": lax.rem(sub + d, 4)}

    def pool_dev(d):
        return {"pool": lax.rem(pool + d, 8)}

    def send(src, dst, ssem, rsem, dev):
        pltpu.make_async_remote_copy(
            src_ref=src, dst_ref=dst, send_sem=ssem, recv_sem=rsem,
            device_id=dev, device_id_type=MESH,
        ).start()

    def wait(ref, sem):
        pltpu.make_async_copy(ref, ref, sem).wait()

    barrier = pltpu.get_barrier_semaphore()
    partners = [up_dev, down_dev, mate_dev]
    partners += [sub_dev(d) for d in range(1, 4)] + [pool_dev(d) for d in range(1, 8)]
    for dev in partners:
        pl.semaphore_signal(barrier, inc=1, device_id=dev, device_id_type=MESH)

    loads = [
        pltpu.make_async_copy(src, dst, load_sem.at[n])
        for n, (src, dst) in enumerate(
            ((q_hbm.at[0], qv), (c_hbm.at[0], cv), (wg_hbm.at[0], wg), (wu_hbm.at[0], wu), (wd_hbm.at[0], wd))
        )
    ]
    for load in loads:
        load.start()

    lane = lax.broadcasted_iota(jnp.int32, (TOK, 128), 1)
    score = score_ref[...]
    weight = ROUTED * score / jnp.sum(score, axis=1, keepdims=True)
    hit = jnp.zeros((TOK, 128), F32)
    mix = jnp.zeros((TOK, 128), F32)
    for k in range(8):
        expert = routes_ref[:, k : k + 1]
        w = weight[:, k : k + 1]
        high = w.astype(BF16).astype(F32)
        hit = hit + jnp.where(lane == expert, 1.0, 0.0)
        mix = mix + jnp.where(lane == expert + 32, high, 0.0)
        mix = mix + jnp.where(lane == expert + 64, w - high, 0.0)
    before = (
        lax.broadcasted_iota(jnp.int32, (TOK, TOK), 1) < lax.broadcasted_iota(jnp.int32, (TOK, TOK), 0)
    )
    earlier = jnp.dot(jnp.where(before, 1.0, 0.0).astype(BF16), hit.astype(BF16), preferred_element_type=F32)
    table = (earlier + 1.0) * hit + mix
    xb[0, 0, 0, 0:TOK, 0:WIDTH] = x_ref[...]
    xb[0, 0, 0, 0:TOK, WIDTH:WIDE] = table.astype(BF16)

    pl.semaphore_wait(barrier, len(partners))

    def rows(i):
        return pl.ds(TOK * i, TOK)

    def pass_up(a, i):
        send(xb.at[0, a, 0, rows(i)], xb.at[0, a + 1, 0, rows(i)], ring_send, ring_recv.at[0, a + 1, i], up_dev)

    def pass_down(a, i):
        send(xb.at[1, a, 0, rows(i)], xb.at[1, a + 1, 0, rows(i)], ring_send, ring_recv.at[1, a + 1, i], down_dev)

    def to_mate(h, a):
        send(xb.at[h, a, 0], xb.at[h, a, 1], mate_send, mate_recv.at[h, a], mate_dev)

    for d in (2, 1, 3):
        send(xb.at[0, 0, 0, rows(0)], xb.at[0, 0, 0, rows(4 - d)], y_send, y_recv.at[4 - d], sub_dev(d))
    for i in (0, 1, 3, 2):
        if i:
            wait(xb.at[0, 0, 0, rows(i)], y_recv.at[i])
        pass_up(0, i)
        send(xb.at[0, 0, 0, rows(i)], xb.at[1, 0, 0, rows(i)], ring_send, ring_recv.at[1, 0, i], down_dev)
    to_mate(0, 0)

    loads[0].wait()
    loads[1].wait()
    entries = cv[...]
    scores = lax.dot_general(qv[...], entries, (((1,), (1,)), ((), ())), preferred_element_type=F32) * SCALE
    valid = lax.broadcasted_iota(jnp.int32, scores.shape, 1) < len_ref[...]
    top = jnp.max(jnp.where(valid, scores, -jnp.inf), axis=1, keepdims=True)
    expo = jnp.where(valid, jnp.exp(scores - top), 0.0)
    probs = (expo / jnp.sum(expo, axis=1, keepdims=True)).astype(BF16)
    ctxv[...] = jnp.dot(probs, entries[:, 0:KV_RANK], preferred_element_type=F32).astype(BF16)
    ctx_out = pltpu.make_async_copy(ctxv, ctx_hbm.at[0], load_sem.at[5])
    ctx_out.start()
    for load in loads[2:]:
        load.wait()

    def placing(h, u):
        tab = xb[h, pl.ds(2 * u, 2), :, :, WIDTH:WIDE].reshape(256, 128).astype(F32)
        lanes = lax.broadcasted_iota(jnp.int32, (256, 128), 1)
        slot = jnp.sum(jnp.where(lanes == peer, tab, 0.0), axis=1, keepdims=True)
        share = jnp.where((lanes == peer + 32) | (lanes == peer + 64), tab, 0.0)
        wt = jnp.sum(share, axis=1, keepdims=True)
        base = lax.broadcasted_iota(jnp.int32, (256, 1), 0) // TOK * MOST - 1
        place = jnp.where(slot > 0.5, slot.astype(jnp.int32) + base, -1)
        onehot = lax.broadcasted_iota(jnp.int32, (256, GROUP), 1) == place
        return jnp.where(onehot, 1.0, 0.0).astype(BF16), wt

    def gates(k):
        u, h = k // 2, lax.rem(k, 2)
        for j in range(2):
            wait(xb.at[h, 2 * u + j, 1], mate_recv.at[h, 2 * u + j])
        onehot, _ = placing(h, u)
        x = xb[h, pl.ds(2 * u, 2), :, :, 0:WIDTH].reshape(256, WIDTH)
        picked = lax.dot_general(onehot, x, (((0,), (0,)), ((), ())), preferred_element_type=F32).astype(BF16)
        gate = jnp.dot(picked, wg[...], preferred_element_type=F32).astype(BF16)
        for n in range(4):
            sp[k, n, :, 0:SHARE] = gate[:, SHARE * n : SHARE * (n + 1)]
        upper = jnp.dot(picked, wu[...], preferred_element_type=F32).astype(BF16)
        for n in range(4):
            sp[k, n, :, SHARE : 2 * SHARE] = upper[:, SHARE * n : SHARE * (n + 1)]

        def give(d):
            c = lax.rem(col + d, 4)
            dest = h * 4 + c
            place = lax.rem(pool - dest + 8, 8) - 1
            send(sp.at[k, c], rp.at[u, place], rp_send, rp_recv.at[u], {"pool": dest})

        for d in (2, 1, 3):
            give(d)

        @pl.when(h != row)
        def _():
            give(0)

    def hidden(u):
        wait(rp.at[u], rp_recv.at[u])
        total = sp[2 * u + row, col].astype(F32)
        for n in range(7):
            total = total + rp[u, n].astype(F32)
        gate, upper = total[:, 0:SHARE], total[:, SHARE : 2 * SHARE]
        hr[u, pool] = (gate / (1.0 + jnp.exp(-gate)) * upper).astype(BF16)
        for d in (6, 2, 5, 7, 3, 1, 4):
            send(hr.at[u, pool], hr.at[u, pool], h_send, h_recv.at[u], pool_dev(d))

    def down(u):
        wait(hr.at[u, 0:7], h_recv.at[u])
        for h in range(2):
            hid = jnp.concatenate([hr[u, 4 * h + n] for n in range(4)], axis=1)
            out = jnp.dot(hid, wd[...], preferred_element_type=F32).astype(BF16)
            onehot, wt = placing(h, u)
            mixed = wt * jnp.dot(onehot, out, preferred_element_type=F32)
            for j in range(2):
                a = 2 * u + j
                cs[h, a] = mixed[128 * j + 64 : 128 * j + 128].astype(BF16)
                send(cs.at[h, a], cm.at[h, a], cm_send, cm_recv.at[h, a], mate_dev)
                co[h, a] = mixed[128 * j : 128 * j + 64]

    def hop(t, _):
        @pl.when(t <= 8)
        def _():
            for i in (0, 1, 3, 2):
                @pl.when(t <= 7)
                def _():
                    wait(xb.at[0, t, 0, rows(i)], ring_recv.at[0, t, i])

                @pl.when(t <= 6)
                def _():
                    pass_up(t, i)

                wait(xb.at[1, t - 1, 0, rows(i)], ring_recv.at[1, t - 1, i])

                @pl.when(t <= 7)
                def _():
                    pass_down(t - 1, i)

            @pl.when(t <= 7)
            def _():
                to_mate(0, t)

            to_mate(1, t - 1)

        @pl.when(t >= 2)
        def _():
            gates(t - 2)

        @pl.when((t >= 5) & (lax.rem(t, 2) == 1))
        def _():
            hidden((t - 5) // 2)

        @pl.when((t >= 7) & (lax.rem(t, 2) == 1))
        def _():
            down((t - 7) // 2)

        return 0

    lax.fori_loop(1, 10, hop, 0)
    hidden(3)
    down(2)
    down(3)

    def own(h, a, i):
        return co[h, a, rows(i)] + cm[h, a, rows(i)].astype(F32)

    def back(h, a, i, dev):
        after = lax.rem(a + 7, 8)
        send(zs.at[h, a, rows(i)], zr.at[h, after, rows(i)], z_send, z_recv.at[h, after, i], dev)

    ways = ((0, down_dev), (1, up_dev))
    order = (2, 1, 3, 0)
    for h, dev in ways:
        wait(cm.at[h, 7], cm_recv.at[h, 7])
    for i in order:
        for h, dev in ways:
            zs[h, 7, rows(i)] = own(h, 7, i).astype(BF16)
            back(h, 7, i, dev)

    def home(s, _):
        a = 6 - s
        for h, dev in ways:
            wait(cm.at[h, a], cm_recv.at[h, a])
        for i in order:
            for h, dev in ways:
                wait(zr.at[h, a, rows(i)], z_recv.at[h, a, i])
                zs[h, a, rows(i)] = (own(h, a, i) + zr[h, a, rows(i)].astype(F32)).astype(BF16)
                back(h, a, i, dev)
        return 0

    lax.fori_loop(0, 6, home, 0)
    for h, dev in ways:
        wait(cm.at[h, 0], cm_recv.at[h, 0])
    total = None
    for i in order:
        wait(zr.at[1, 0, rows(i)], z_recv.at[1, 0, i])
        zs[1, 0, rows(i)] = (own(1, 0, i) + zr[1, 0, rows(i)].astype(F32)).astype(BF16)
        back(1, 0, i, up_dev)
    for i in order:
        wait(zr.at[0, 0, rows(i)], z_recv.at[0, 0, i])
        wait(zr.at[1, 7, rows(i)], z_recv.at[1, 7, i])
        total = own(0, 0, i) + zr[0, 0, rows(i)].astype(F32) + zr[1, 7, rows(i)].astype(F32)
        if i:
            fs[i - 1] = total.astype(BF16)
            send(fs.at[i - 1], yr.at[i - 1], f_send, f_recv, sub_dev(i))

    ctx_out.wait()
    wait(xb.at[0, 0, 0, 0 : 3 * TOK], y_send)
    wait(xb.at[0, 0:7, 0], ring_send)
    wait(xb.at[1, :, 0], ring_send)
    wait(xb.at[0, :, 0], mate_send)
    wait(xb.at[1, :, 0], mate_send)
    wait(rp, rp_send)
    for u in range(4):
        wait(hr.at[u, 0:7], h_send)
    wait(cs, cm_send)
    wait(zs.at[0, 0:7], z_send)
    wait(zs.at[1], z_send)
    wait(fs, f_send)

    wait(yr, f_recv)
    for n in range(3):
        total = total + yr[n].astype(F32)
    moe_ref[...] = total.astype(BF16)


def per_device(x_a, routes, route_score, w_gate, w_up, w_down, queries, cache, lengths):
    vmem = pl.BlockSpec(memory_space=pltpu.VMEM)
    hbm = pl.BlockSpec(memory_space=pl.ANY)
    dma, dmas = pltpu.SemaphoreType.DMA, lambda *s: pltpu.SemaphoreType.DMA(s)
    return pl.pallas_call(
        kernel,
        out_shape=(
            jax.ShapeDtypeStruct((TOK, WIDTH), BF16),
            jax.ShapeDtypeStruct((1, 128, KV_RANK), BF16),
        ),
        in_specs=[vmem] * 4 + [hbm] * 5,
        out_specs=(vmem, hbm),
        scratch_shapes=[
            pltpu.VMEM((2, 8, 2, 64, WIDE), BF16),
            pltpu.VMEM((WIDTH, FFS), BF16),
            pltpu.VMEM((WIDTH, FFS), BF16),
            pltpu.VMEM((FFS, WIDTH), BF16),
            pltpu.VMEM((128, 576), BF16),
            pltpu.VMEM((128, 576), BF16),
            pltpu.VMEM((128, KV_RANK), BF16),
            pltpu.VMEM((8, 4, GROUP, 2 * SHARE), BF16),
            pltpu.VMEM((4, 7, GROUP, 2 * SHARE), BF16),
            pltpu.VMEM((4, 8, GROUP, SHARE), BF16),
            pltpu.VMEM((2, 8, 64, WIDTH), F32),
            pltpu.VMEM((2, 8, 64, WIDTH), BF16),
            pltpu.VMEM((2, 8, 64, WIDTH), BF16),
            pltpu.VMEM((2, 8, 64, WIDTH), BF16),
            pltpu.VMEM((2, 8, 64, WIDTH), BF16),
            pltpu.VMEM((3, TOK, WIDTH), BF16),
            pltpu.VMEM((3, TOK, WIDTH), BF16),
            dmas(6), dma, dmas(4), dma, dmas(2, 8, 4), dma, dmas(2, 8),
            dma, dmas(4), dma, dmas(4), dma, dmas(2, 8), dma, dmas(2, 8, 4), dma, dma,
        ],
        compiler_params=pltpu.CompilerParams(
            collective_id=0, has_side_effects=True, vmem_limit_bytes=48 << 20
        ),
        name="moe_attention",
    )(x_a, routes, route_score, lengths.reshape(1, 1), w_gate, w_up, w_down, queries, cache)


def solution(mesh):
    placed = (
        P(("peer", "sub"), "pool"),
        P(("peer", "sub"), None),
        P(("peer", "sub"), None),
        P("peer", "pool", "sub"),
        P("peer", "pool", "sub"),
        P("peer", "sub", "pool"),
        P(("pool", "peer", "sub"), None, None),
        P(("pool", "peer", "sub"), None, None),
        P(("pool", "peer", "sub")),
    )
    return jax.shard_map(
        per_device,
        mesh=mesh,
        in_specs=placed,
        out_specs=(P(("peer", "sub"), "pool"), P(("pool", "peer", "sub"), None, None)),
        check_vma=False,
    )
```

```python
import functools

import jax
import jax.numpy as jnp
from jax import lax
from jax.experimental import pallas as pl
from jax.experimental.pallas import tpu as pltpu
from jax.sharding import PartitionSpec as P

KV_RANK = 512
SCALE = 192 ** (-0.5)
ROUTED = 2.5
TOK = 16
MOST = 5
WIDTH = 896
WIDE = 1024
FFS = 512
HALF = 8 * MOST
GROUP = 2 * HALF
PAD = 48
SHARE = FFS // 4
MESH = pl.DeviceIdType.MESH
F32, BF16 = jnp.float32, jnp.bfloat16


def kernel(
    x_ref, routes_ref, score_ref, len_ref, wg_hbm, wu_hbm, wd_hbm, q_hbm, c_hbm,
    moe_ref, ctx_hbm,
    xb, wg, wu, wd, qv, cv, ctxv, po, pm, pr, sp, rp, hr, yo, ym, ye, co, zs, zr, fs, yr,
    load_sem, y_send, y_recv, ring_send, ring_recv, mate_send, mate_recv,
    rp_send, rp_recv, h_send, h_recv, ym_send, ym_recv, z_send, z_recv, f_send, f_recv,
):
    pool, peer, sub = lax.axis_index("pool"), lax.axis_index("peer"), lax.axis_index("sub")
    row, col = pool // 4, lax.rem(pool, 4)
    up_dev = {"peer": lax.rem(peer + 2, 32)}
    down_dev = {"peer": lax.rem(peer + 30, 32)}
    mate_dev = {"peer": peer + 1 - 2 * lax.rem(peer, 2)}

    def sub_dev(d):
        return {"sub": lax.rem(sub + d, 4)}

    def pool_dev(d):
        return {"pool": lax.rem(pool + d, 8)}

    def send(src, dst, ssem, rsem, dev):
        pltpu.make_async_remote_copy(
            src_ref=src, dst_ref=dst, send_sem=ssem, recv_sem=rsem,
            device_id=dev, device_id_type=MESH,
        ).start()

    def wait(ref, sem):
        pltpu.make_async_copy(ref, ref, sem).wait()

    barrier = pltpu.get_barrier_semaphore()
    partners = [up_dev, down_dev, mate_dev]
    partners += [sub_dev(d) for d in range(1, 4)] + [pool_dev(d) for d in range(1, 8)]
    for dev in partners:
        pl.semaphore_signal(barrier, inc=1, device_id=dev, device_id_type=MESH)

    loads = [
        pltpu.make_async_copy(src, dst, load_sem.at[n])
        for n, (src, dst) in enumerate(
            ((q_hbm.at[0], qv), (c_hbm.at[0], cv), (wg_hbm.at[0], wg), (wu_hbm.at[0], wu), (wd_hbm.at[0], wd))
        )
    ]
    for load in loads:
        load.start()

    lane = lax.broadcasted_iota(jnp.int32, (TOK, 128), 1)
    score = score_ref[...]
    weight = ROUTED * score / jnp.sum(score, axis=0, keepdims=True)
    high = weight.astype(BF16)
    eye = lax.broadcasted_iota(jnp.int32, (8, 8), 0) == lax.broadcasted_iota(jnp.int32, (8, 8), 1)
    eye = jnp.where(eye, 1.0, 0.0).astype(BF16)

    def turn(v):
        return lax.dot_general(v, eye, (((0,), (0,)), ((), ())), preferred_element_type=F32)

    names = turn(routes_ref[...].astype(F32).astype(BF16)).astype(jnp.int32)
    low = turn((weight - high.astype(F32)).astype(BF16))
    high = turn(high)
    hit = jnp.zeros((TOK, 128), F32)
    mix = jnp.zeros((TOK, 128), F32)
    for k in range(8):
        expert = names[:, k : k + 1]
        hit = hit + jnp.where(lane == expert, 1.0, 0.0)
        mix = mix + jnp.where(lane == expert + 32, high[:, k : k + 1], 0.0)
        mix = mix + jnp.where(lane == expert + 64, low[:, k : k + 1], 0.0)
    before = (
        lax.broadcasted_iota(jnp.int32, (TOK, TOK), 1) < lax.broadcasted_iota(jnp.int32, (TOK, TOK), 0)
    )
    earlier = jnp.dot(jnp.where(before, 1.0, 0.0).astype(BF16), hit.astype(BF16), preferred_element_type=F32)
    table = (earlier + 1.0) * hit + mix
    xb[0, 0, 0:TOK, 0:WIDTH] = x_ref[...]
    xb[0, 0, 0:TOK, WIDTH:WIDE] = table.astype(BF16)

    pl.semaphore_wait(barrier, len(partners))

    def rows(i):
        return pl.ds(TOK * i, TOK)

    def pass_up(a, i):
        send(xb.at[0, a, rows(i)], xb.at[0, a + 1, rows(i)], ring_send, ring_recv.at[0, a + 1, i], up_dev)

    def pass_down(a, i):
        send(xb.at[1, a, rows(i)], xb.at[1, a + 1, rows(i)], ring_send, ring_recv.at[1, a + 1, i], down_dev)

    for d in (2, 1, 3):
        send(xb.at[0, 0, rows(0)], xb.at[0, 0, rows(4 - d)], y_send, y_recv.at[4 - d], sub_dev(d))
    for i in (0, 1, 3, 2):
        if i:
            wait(xb.at[0, 0, rows(i)], y_recv.at[i])
        pass_up(0, i)
        send(xb.at[0, 0, rows(i)], xb.at[1, 0, rows(i)], ring_send, ring_recv.at[1, 0, i], down_dev)

    ctx_out = pltpu.make_async_copy(ctxv, ctx_hbm.at[0], load_sem.at[5])

    def attention():
        loads[0].wait()
        loads[1].wait()
        entries = cv[...]
        scores = lax.dot_general(qv[...], entries, (((0,), (0,)), ((), ())), preferred_element_type=F32) * SCALE
        valid = lax.broadcasted_iota(jnp.int32, scores.shape, 1) < len_ref[...]
        top = jnp.max(jnp.where(valid, scores, -jnp.inf), axis=1, keepdims=True)
        expo = jnp.where(valid, jnp.exp(scores - top), 0.0)
        probs = (expo / jnp.sum(expo, axis=1, keepdims=True)).astype(BF16)
        ctxv[...] = lax.dot_general(
            probs, entries[0:KV_RANK], (((1,), (1,)), ((), ())), preferred_element_type=F32
        ).astype(BF16)
        ctx_out.start()

    for load in loads[2:]:
        load.wait()

    def placing(k, expert, first):
        u, h = k // 2, lax.rem(k, 2)
        tab = xb[h, pl.ds(2 * u, 2), :, WIDTH:WIDE].reshape(128, 128).astype(F32)
        lanes = lax.broadcasted_iota(jnp.int32, (128, 128), 1)
        slot = jnp.sum(jnp.where(lanes == expert, tab, 0.0), axis=1, keepdims=True)
        share = jnp.where((lanes == expert + 32) | (lanes == expert + 64), tab, 0.0)
        base = lax.broadcasted_iota(jnp.int32, (128, 1), 0) // TOK * MOST - 1 + first
        place = jnp.where(slot > 0.5, slot.astype(jnp.int32) + base, -1)
        return place, jnp.sum(share, axis=1, keepdims=True)

    mate = peer + 1 - 2 * lax.rem(peer, 2)

    def select(k):
        u, h = k // 2, lax.rem(k, 2)
        mine, _ = placing(k, peer, 0)
        other, _ = placing(k, mate, PAD)
        slots = lax.broadcasted_iota(jnp.int32, (128, 128), 1)
        onehot = jnp.where((slots == mine) | (slots == other), 1.0, 0.0).astype(BF16)
        x = xb[h, pl.ds(2 * u, 2), :, 0:WIDTH].reshape(128, WIDTH)
        picked = lax.dot_general(onehot, x, (((0,), (0,)), ((), ())), preferred_element_type=F32).astype(BF16)
        pm[k] = picked[PAD : 2 * PAD]
        send(pm.at[k], pr.at[k], mate_send, mate_recv.at[k], mate_dev)
        po[k] = picked[0:PAD]

    def gates(k):
        u, h = k // 2, lax.rem(k, 2)
        wait(pr.at[k], mate_recv.at[k])
        picked = jnp.concatenate([po[k].astype(F32)[0:HALF], pr[k].astype(F32)[0:HALF]], axis=0).astype(BF16)
        gate = jnp.dot(picked, wg[...], preferred_element_type=F32).astype(BF16)
        for n in range(4):
            sp[k, n, :, 0:SHARE] = gate[:, SHARE * n : SHARE * (n + 1)]
        upper = jnp.dot(picked, wu[...], preferred_element_type=F32).astype(BF16)
        for n in range(4):
            sp[k, n, :, SHARE : 2 * SHARE] = upper[:, SHARE * n : SHARE * (n + 1)]

        def give(d):
            c = lax.rem(col + d, 4)
            dest = h * 4 + c
            place = lax.rem(pool - dest + 8, 8) - 1
            send(sp.at[k, c], rp.at[u, place], rp_send, rp_recv.at[u], {"pool": dest})

        for d in (2, 1, 3):
            give(d)

        @pl.when(h != row)
        def _():
            give(0)

    def hidden(u):
        wait(rp.at[u], rp_recv.at[u])
        total = sp[2 * u + row, col].astype(F32)
        for n in range(7):
            total = total + rp[u, n].astype(F32)
        gate, upper = total[:, 0:SHARE], total[:, SHARE : 2 * SHARE]
        hr[u, pool] = (gate / (1.0 + jnp.exp(-gate)) * upper).astype(BF16)
        for d in (6, 2, 5, 7, 3, 1, 4):
            send(hr.at[u, pool], hr.at[u, pool], h_send, h_recv.at[u], pool_dev(d))

    def down(u):
        wait(hr.at[u, 0:7], h_recv.at[u])
        for h in range(2):
            k = 2 * u + h
            hid = jnp.concatenate([hr[u, 4 * h + n] for n in range(4)], axis=1)
            out = jnp.dot(hid, wd[...], preferred_element_type=F32)
            none = jnp.zeros((PAD - HALF, WIDTH), F32)
            ym[k] = jnp.concatenate([out[HALF:GROUP], none], axis=0).astype(BF16)
            send(ym.at[k], ye.at[k], ym_send, ym_recv.at[k], mate_dev)
            yo[k] = jnp.concatenate([out[0:HALF], none], axis=0).astype(BF16)

    def combine(k):
        u, h = k // 2, lax.rem(k, 2)
        wait(ye.at[k], ym_recv.at[k])
        slots = lax.broadcasted_iota(jnp.int32, (128, PAD), 1)
        total = None
        for expert, part in ((peer, yo), (mate, ye)):
            place, wt = placing(k, expert, 0)
            onehot = jnp.where(slots == place, 1.0, 0.0).astype(BF16)
            term = wt * jnp.dot(onehot, part[k], preferred_element_type=F32)
            total = term if total is None else total + term
        co[h, pl.ds(2 * u, 2)] = total.reshape(2, 64, WIDTH)

    def hop(t, _):
        @pl.when(t <= 8)
        def _():
            for i in (0, 1, 3, 2):
                @pl.when(t <= 7)
                def _():
                    wait(xb.at[0, t, rows(i)], ring_recv.at[0, t, i])

                @pl.when(t <= 6)
                def _():
                    pass_up(t, i)

                wait(xb.at[1, t - 1, rows(i)], ring_recv.at[1, t - 1, i])

                @pl.when(t <= 7)
                def _():
                    pass_down(t - 1, i)

            select(t - 1)

        @pl.when(t >= 2)
        def _():
            gates(t - 2)

        @pl.when((t >= 5) & (lax.rem(t, 2) == 1))
        def _():
            hidden((t - 5) // 2)

        @pl.when((t >= 7) & (lax.rem(t, 2) == 1))
        def _():
            down((t - 7) // 2)

        return 0

    lax.fori_loop(1, 10, hop, 0)
    attention()
    hidden(3)
    down(2)

    def mixes(k, _):
        combine(k)
        return 0

    lax.fori_loop(0, 4, mixes, 0)
    down(3)
    lax.fori_loop(4, 8, mixes, 0)

    def own(h, a, i):
        return co[h, a, rows(i)]

    def back(h, a, i, dev):
        after = lax.rem(a + 7, 8)
        send(zs.at[h, a, rows(i)], zr.at[h, after, rows(i)], z_send, z_recv.at[h, after, i], dev)

    ways = ((0, down_dev), (1, up_dev))
    order = (2, 1, 3, 0)
    for i in order:
        for h, dev in ways:
            zs[h, 7, rows(i)] = own(h, 7, i).astype(BF16)
            back(h, 7, i, dev)

    def home(s, _):
        a = 6 - s
        for i in order:
            for h, dev in ways:
                wait(zr.at[h, a, rows(i)], z_recv.at[h, a, i])
                zs[h, a, rows(i)] = (own(h, a, i) + zr[h, a, rows(i)].astype(F32)).astype(BF16)
                back(h, a, i, dev)
        return 0

    lax.fori_loop(0, 6, home, 0)
    total = None
    for i in order:
        wait(zr.at[1, 0, rows(i)], z_recv.at[1, 0, i])
        zs[1, 0, rows(i)] = (own(1, 0, i) + zr[1, 0, rows(i)].astype(F32)).astype(BF16)
        back(1, 0, i, up_dev)
    for i in order:
        wait(zr.at[0, 0, rows(i)], z_recv.at[0, 0, i])
        wait(zr.at[1, 7, rows(i)], z_recv.at[1, 7, i])
        total = own(0, 0, i) + zr[0, 0, rows(i)].astype(F32) + zr[1, 7, rows(i)].astype(F32)
        if i:
            fs[i - 1] = total.astype(BF16)
            send(fs.at[i - 1], yr.at[i - 1], f_send, f_recv, sub_dev(i))

    ctx_out.wait()
    wait(xb.at[0, 0, 0 : 3 * TOK], y_send)
    wait(xb.at[0, 0:7], ring_send)
    wait(xb.at[1], ring_send)
    wait(pm, mate_send)
    wait(rp, rp_send)
    for u in range(4):
        wait(hr.at[u, 0:7], h_send)
    wait(ym, ym_send)
    wait(zs.at[0, 0:7], z_send)
    wait(zs.at[1], z_send)
    wait(fs, f_send)

    wait(yr, f_recv)
    for n in range(3):
        total = total + yr[n].astype(F32)
    moe_ref[...] = total.astype(BF16)


def per_device(x_a, routes, route_score, w_gate, w_up, w_down, queries, cache, lengths):
    vmem = pl.BlockSpec(memory_space=pltpu.VMEM)
    hbm = pl.BlockSpec(memory_space=pltpu.HBM)
    dma, dmas = pltpu.SemaphoreType.DMA, lambda *s: pltpu.SemaphoreType.DMA(s)
    return pl.pallas_call(
        kernel,
        out_shape=(
            jax.ShapeDtypeStruct((TOK, WIDTH), BF16),
            jax.ShapeDtypeStruct((1, 128, KV_RANK), BF16),
        ),
        in_specs=[vmem] * 4 + [hbm] * 5,
        out_specs=(vmem, hbm),
        scratch_shapes=[
            pltpu.VMEM((2, 8, 64, WIDE), BF16),
            pltpu.VMEM((WIDTH, FFS), BF16),
            pltpu.VMEM((WIDTH, FFS), BF16),
            pltpu.VMEM((FFS, WIDTH), BF16),
            pltpu.VMEM((576, 128), BF16),
            pltpu.VMEM((576, 128), BF16),
            pltpu.VMEM((128, KV_RANK), BF16),
            pltpu.VMEM((8, PAD, WIDTH), BF16),
            pltpu.VMEM((8, PAD, WIDTH), BF16),
            pltpu.VMEM((8, PAD, WIDTH), BF16),
            pltpu.VMEM((8, 4, GROUP, 2 * SHARE), BF16),
            pltpu.VMEM((4, 7, GROUP, 2 * SHARE), BF16),
            pltpu.VMEM((4, 8, GROUP, SHARE), BF16),
            pltpu.VMEM((8, PAD, WIDTH), BF16),
            pltpu.VMEM((8, PAD, WIDTH), BF16),
            pltpu.VMEM((8, PAD, WIDTH), BF16),
            pltpu.VMEM((2, 8, 64, WIDTH), F32),
            pltpu.VMEM((2, 8, 64, WIDTH), BF16),
            pltpu.VMEM((2, 8, 64, WIDTH), BF16),
            pltpu.VMEM((3, TOK, WIDTH), BF16),
            pltpu.VMEM((3, TOK, WIDTH), BF16),
            dmas(6), dma, dmas(4), dma, dmas(2, 8, 4), dma, dmas(8),
            dma, dmas(4), dma, dmas(4), dma, dmas(8), dma, dmas(2, 8, 4), dma, dma,
        ],
        compiler_params=pltpu.CompilerParams(
            collective_id=0, has_side_effects=True, vmem_limit_bytes=255 << 18
        ),
        name="moe_attention",
    )(
        x_a, routes.T, route_score.T, lengths.reshape(1, 1), w_gate, w_up, w_down,
        jnp.swapaxes(queries, 1, 2), jnp.swapaxes(cache, 1, 2),
    )


def solution(mesh):
    placed = (
        P(("peer", "sub"), "pool"),
        P(("peer", "sub"), None),
        P(("peer", "sub"), None),
        P("peer", "pool", "sub"),
        P("peer", "pool", "sub"),
        P("peer", "sub", "pool"),
        P(("pool", "peer", "sub"), None, None),
        P(("pool", "peer", "sub"), None, None),
        P(("pool", "peer", "sub")),
    )
    return jax.shard_map(
        per_device,
        mesh=mesh,
        in_specs=placed,
        out_specs=(P(("peer", "sub"), "pool"), P(("pool", "peer", "sub"), None, None)),
        check_vma=False,
    )
```

```python
import functools

import jax
import jax.numpy as jnp
from jax import lax
from jax.experimental import pallas as pl
from jax.experimental.pallas import tpu as pltpu
from jax.sharding import PartitionSpec as P

KV_RANK = 512
SCALE = 192 ** (-0.5)
ROUTED = 2.5
TOK = 16
MOST = 5
WIDTH = 896
WIDE = 1024
FFS = 512
HALF = 8 * MOST
GROUP = 2 * HALF
PAD = 48
SHARE = FFS // 4
MESH = pl.DeviceIdType.MESH
F32, BF16 = jnp.float32, jnp.bfloat16


def kernel(
    x_ref, routes_ref, score_ref, len_ref, wg_hbm, wu_hbm, wd_hbm, q_hbm, c_hbm,
    moe_ref, ctx_hbm,
    xb, wg, wu, wd, qv, cv, ctxv, po, pm, pr, pk, sp, rp, hr, yo, ym, ye, co, zs, zr, fs, yr,
    load_sem, y_send, y_recv, ring_send, ring_recv, mate_send, mate_recv,
    rp_send, rp_recv, h_send, h_recv, ym_send, ym_recv, z_send, z_recv, f_send, f_recv,
):
    pool, peer, sub = lax.axis_index("pool"), lax.axis_index("peer"), lax.axis_index("sub")
    row, col = pool // 4, lax.rem(pool, 4)
    up_dev = {"peer": lax.rem(peer + 2, 32)}
    down_dev = {"peer": lax.rem(peer + 30, 32)}
    mate_dev = {"peer": peer + 1 - 2 * lax.rem(peer, 2)}

    def sub_dev(d):
        return {"sub": lax.rem(sub + d, 4)}

    def pool_dev(d):
        return {"pool": lax.rem(pool + d, 8)}

    def send(src, dst, ssem, rsem, dev):
        pltpu.make_async_remote_copy(
            src_ref=src, dst_ref=dst, send_sem=ssem, recv_sem=rsem,
            device_id=dev, device_id_type=MESH,
        ).start()

    def wait(ref, sem):
        pltpu.make_async_copy(ref, ref, sem).wait()

    barrier = pltpu.get_barrier_semaphore()
    partners = [up_dev, down_dev, mate_dev]
    partners += [sub_dev(d) for d in range(1, 4)] + [pool_dev(d) for d in range(1, 8)]
    for dev in partners:
        pl.semaphore_signal(barrier, inc=1, device_id=dev, device_id_type=MESH)

    loads = [
        pltpu.make_async_copy(src, dst, load_sem.at[n])
        for n, (src, dst) in enumerate(
            ((q_hbm.at[0], qv), (c_hbm.at[0], cv), (wg_hbm.at[0], wg), (wu_hbm.at[0], wu), (wd_hbm.at[0], wd))
        )
    ]
    for load in loads:
        load.start()

    lane = lax.broadcasted_iota(jnp.int32, (TOK, 128), 1)
    score = score_ref[...]
    weight = ROUTED * score / jnp.sum(score, axis=0, keepdims=True)
    high = weight.astype(BF16)
    eye = lax.broadcasted_iota(jnp.int32, (8, 8), 0) == lax.broadcasted_iota(jnp.int32, (8, 8), 1)
    eye = jnp.where(eye, 1.0, 0.0).astype(BF16)

    def turn(v):
        return lax.dot_general(v, eye, (((0,), (0,)), ((), ())), preferred_element_type=F32)

    names = turn(routes_ref[...].astype(F32).astype(BF16)).astype(jnp.int32)
    low = turn((weight - high.astype(F32)).astype(BF16))
    high = turn(high)
    hit = jnp.zeros((TOK, 128), F32)
    mix = jnp.zeros((TOK, 128), F32)
    for k in range(8):
        expert = names[:, k : k + 1]
        hit = hit + jnp.where(lane == expert, 1.0, 0.0)
        mix = mix + jnp.where(lane == expert + 32, high[:, k : k + 1], 0.0)
        mix = mix + jnp.where(lane == expert + 64, low[:, k : k + 1], 0.0)
    before = (
        lax.broadcasted_iota(jnp.int32, (TOK, TOK), 1) < lax.broadcasted_iota(jnp.int32, (TOK, TOK), 0)
    )
    earlier = jnp.dot(jnp.where(before, 1.0, 0.0).astype(BF16), hit.astype(BF16), preferred_element_type=F32)
    table = (earlier + 1.0) * hit + mix
    xb[0, 0, 0:TOK, 0:WIDTH] = x_ref[...]
    xb[0, 0, 0:TOK, WIDTH:WIDE] = table.astype(BF16)

    pl.semaphore_wait(barrier, len(partners))

    def rows(i):
        return pl.ds(TOK * i, TOK)

    def pass_up(a, i):
        send(xb.at[0, a, rows(i)], xb.at[0, a + 1, rows(i)], ring_send, ring_recv.at[0, a + 1, i], up_dev)

    def pass_down(a, i):
        send(xb.at[1, a, rows(i)], xb.at[1, a + 1, rows(i)], ring_send, ring_recv.at[1, a + 1, i], down_dev)

    for d in (2, 1, 3):
        send(xb.at[0, 0, rows(0)], xb.at[0, 0, rows(4 - d)], y_send, y_recv.at[4 - d], sub_dev(d))
    for i in (0, 1, 3, 2):
        if i:
            wait(xb.at[0, 0, rows(i)], y_recv.at[i])
        pass_up(0, i)
        send(xb.at[0, 0, rows(i)], xb.at[1, 0, rows(i)], ring_send, ring_recv.at[1, 0, i], down_dev)

    ctx_out = pltpu.make_async_copy(ctxv, ctx_hbm.at[0], load_sem.at[5])

    def attention():
        loads[0].wait()
        loads[1].wait()
        entries = cv[...]
        scores = lax.dot_general(qv[...], entries, (((0,), (0,)), ((), ())), preferred_element_type=F32) * SCALE
        valid = lax.broadcasted_iota(jnp.int32, scores.shape, 1) < len_ref[...]
        top = jnp.max(jnp.where(valid, scores, -jnp.inf), axis=1, keepdims=True)
        expo = jnp.where(valid, jnp.exp(scores - top), 0.0)
        probs = (expo / jnp.sum(expo, axis=1, keepdims=True)).astype(BF16)
        ctxv[...] = lax.dot_general(
            probs, entries[0:KV_RANK], (((1,), (1,)), ((), ())), preferred_element_type=F32
        ).astype(BF16)
        ctx_out.start()

    for load in loads[2:]:
        load.wait()

    def placing(k, expert, first):
        u, h = k // 2, lax.rem(k, 2)
        tab = xb[h, pl.ds(2 * u, 2), :, WIDTH:WIDE].reshape(128, 128).astype(F32)
        lanes = lax.broadcasted_iota(jnp.int32, (128, 128), 1)
        slot = jnp.sum(jnp.where(lanes == expert, tab, 0.0), axis=1, keepdims=True)
        share = jnp.where((lanes == expert + 32) | (lanes == expert + 64), tab, 0.0)
        base = lax.broadcasted_iota(jnp.int32, (128, 1), 0) // TOK * MOST - 1 + first
        place = jnp.where(slot > 0.5, slot.astype(jnp.int32) + base, -1)
        return place, jnp.sum(share, axis=1, keepdims=True)

    mate = peer + 1 - 2 * lax.rem(peer, 2)

    def select(k):
        u, h = k // 2, lax.rem(k, 2)
        mine, _ = placing(k, peer, 0)
        other, _ = placing(k, mate, PAD)
        slots = lax.broadcasted_iota(jnp.int32, (128, 128), 1)
        onehot = jnp.where((slots == mine) | (slots == other), 1.0, 0.0).astype(BF16)
        x = xb[h, pl.ds(2 * u, 2), :, 0:WIDTH].reshape(128, WIDTH)
        picked = lax.dot_general(onehot, x, (((0,), (0,)), ((), ())), preferred_element_type=F32).astype(BF16)
        pm[k] = picked[PAD : 2 * PAD]
        send(pm.at[k], pr.at[k], mate_send, mate_recv.at[k], mate_dev)
        po[k] = picked[0:PAD]

    def gates(k):
        wait(pr.at[k], mate_recv.at[k])
        pk[...] = jnp.concatenate([po[k].astype(F32)[0:HALF], pr[k].astype(F32)[0:HALF]], axis=0).astype(BF16)
        gate = jnp.dot(pk[...], wg[...], preferred_element_type=F32).astype(BF16)
        for n in range(4):
            sp[k, n, :, 0:SHARE] = gate[:, SHARE * n : SHARE * (n + 1)]

    def uppers(k):
        u, h = k // 2, lax.rem(k, 2)
        upper = jnp.dot(pk[...], wu[...], preferred_element_type=F32).astype(BF16)
        for n in range(4):
            sp[k, n, :, SHARE : 2 * SHARE] = upper[:, SHARE * n : SHARE * (n + 1)]

        def give(d):
            c = lax.rem(col + d, 4)
            dest = h * 4 + c
            place = lax.rem(pool - dest + 8, 8) - 1
            send(sp.at[k, c], rp.at[u, place], rp_send, rp_recv.at[u], {"pool": dest})

        for d in (2, 1, 3):
            give(d)

        @pl.when(h != row)
        def _():
            give(0)

    def hidden(u):
        wait(rp.at[u], rp_recv.at[u])
        total = sp[2 * u + row, col].astype(F32)
        for n in range(7):
            total = total + rp[u, n].astype(F32)
        gate, upper = total[:, 0:SHARE], total[:, SHARE : 2 * SHARE]
        hr[u, pool] = (gate / (1.0 + jnp.exp(-gate)) * upper).astype(BF16)
        for d in (6, 2, 5, 7, 3, 1, 4):
            send(hr.at[u, pool], hr.at[u, pool], h_send, h_recv.at[u], pool_dev(d))

    def down(u):
        wait(hr.at[u, 0:7], h_recv.at[u])
        for h in range(2):
            k = 2 * u + h
            hid = jnp.concatenate([hr[u, 4 * h + n] for n in range(4)], axis=1)
            out = jnp.dot(hid, wd[...], preferred_element_type=F32)
            none = jnp.zeros((PAD - HALF, WIDTH), F32)
            ym[k] = jnp.concatenate([out[HALF:GROUP], none], axis=0).astype(BF16)
            send(ym.at[k], ye.at[k], ym_send, ym_recv.at[k], mate_dev)
            yo[k] = jnp.concatenate([out[0:HALF], none], axis=0).astype(BF16)

    def combine(k):
        u, h = k // 2, lax.rem(k, 2)
        wait(ye.at[k], ym_recv.at[k])
        slots = lax.broadcasted_iota(jnp.int32, (128, PAD), 1)
        total = None
        for expert, part in ((peer, yo), (mate, ye)):
            place, wt = placing(k, expert, 0)
            onehot = jnp.where(slots == place, 1.0, 0.0).astype(BF16)
            term = wt * jnp.dot(onehot, part[k], preferred_element_type=F32)
            total = term if total is None else total + term
        co[h, pl.ds(2 * u, 2)] = total.reshape(2, 64, WIDTH)

    above, below = (2, 1), (3, 0)

    def hop(t, _):
        for n, i in enumerate((0, 1, 3, 2)):
            @pl.when(t <= 7)
            def _():
                wait(xb.at[0, t, rows(i)], ring_recv.at[0, t, i])

            @pl.when(t <= (7 if i in above else 6))
            def _():
                way, place = t // 7, jnp.minimum(t + 1, 7)
                send(xb.at[0, t, rows(i)], xb.at[way, place, rows(i)], ring_send, ring_recv.at[way, place, i], up_dev)

            wait(xb.at[1, t - 1, rows(i)], ring_recv.at[1, t - 1, i])

            @pl.when(t <= (6 if i in above else 7))
            def _():
                pass_down(t - 1, i)

            if n == 0:
                @pl.when(t >= 3)
                def _():
                    gates(t - 3)
            elif n == 1:
                @pl.when(t >= 3)
                def _():
                    uppers(t - 3)
            elif n == 2:
                @pl.when((t == 6) | (t == 8))
                def _():
                    hidden((t - 6) // 2)
            else:
                @pl.when(t >= 2)
                def _():
                    select(t - 2)

        return 0

    lax.fori_loop(1, 9, hop, 0)
    select(7)

    def last(k, _):
        gates(k)
        uppers(k)
        return 0

    lax.fori_loop(6, 8, last, 0)

    def mixes(k, _):
        combine(k)
        return 0

    def downs(u, _):
        down(u)
        return 0

    attention()
    hidden(2)
    lax.fori_loop(0, 2, downs, 0)
    hidden(3)
    down(2)
    lax.fori_loop(0, 4, mixes, 0)
    down(3)
    lax.fori_loop(4, 8, mixes, 0)

    def back(h, a, i, way, place):
        send(
            zs.at[h, a, rows(i)], zr.at[way, place, rows(i)], z_send, z_recv.at[way, place, i],
            down_dev if way == 0 else up_dev,
        )

    def start(h, a, i, way, place):
        zs[h, a, rows(i)] = co[h, a, rows(i)].astype(BF16)
        back(h, a, i, way, place)

    def onward(h, a, i):
        wait(zr.at[h, a, rows(i)], z_recv.at[h, a, i])
        zs[h, a, rows(i)] = (co[h, a, rows(i)] + zr[h, a, rows(i)].astype(F32)).astype(BF16)
        back(h, a, i, h, lax.rem(a + 7, 8))

    order = (2, 3, 1, 0)
    for i in order:
        if i in above:
            start(1, 7, i, 0, 7)
            start(1, 6, i, 1, 5)
        else:
            start(0, 7, i, 0, 6)
            start(1, 7, i, 1, 6)

    def home(s, _):
        for i in order:
            if i in above:
                onward(0, 8 - s, i)
                onward(1, 6 - s, i)
            else:
                onward(0, 7 - s, i)
                onward(1, 7 - s, i)
        return 0

    lax.fori_loop(1, 7, home, 0)
    for i in order:
        if i in above:
            onward(0, 1, i)
        else:
            onward(1, 0, i)
    total = None
    for i in order:
        wait(zr.at[0, 0, rows(i)], z_recv.at[0, 0, i])
        wait(zr.at[1, 7, rows(i)], z_recv.at[1, 7, i])
        total = co[0, 0, rows(i)] + zr[0, 0, rows(i)].astype(F32) + zr[1, 7, rows(i)].astype(F32)
        if i:
            fs[i - 1] = total.astype(BF16)
            send(fs.at[i - 1], yr.at[i - 1], f_send, f_recv, sub_dev(i))

    ctx_out.wait()
    wait(xb.at[0, 0, 0 : 3 * TOK], y_send)
    wait(xb.at[0, 0:7], ring_send)
    wait(xb.at[1], ring_send)
    wait(pm, mate_send)
    wait(rp, rp_send)
    for u in range(4):
        wait(hr.at[u, 0:7], h_send)
    wait(ym, ym_send)
    wait(zs.at[0, 0:7], z_send)
    wait(zs.at[1], z_send)
    wait(fs, f_send)

    wait(yr, f_recv)
    for n in range(3):
        total = total + yr[n].astype(F32)
    moe_ref[...] = total.astype(BF16)


def per_device(x_a, routes, route_score, w_gate, w_up, w_down, queries, cache, lengths):
    vmem = pl.BlockSpec(memory_space=pltpu.VMEM)
    hbm = pl.BlockSpec(memory_space=pltpu.HBM)
    dma, dmas = pltpu.SemaphoreType.DMA, lambda *s: pltpu.SemaphoreType.DMA(s)
    return pl.pallas_call(
        kernel,
        out_shape=(
            jax.ShapeDtypeStruct((TOK, WIDTH), BF16),
            jax.ShapeDtypeStruct((1, 128, KV_RANK), BF16),
        ),
        in_specs=[vmem] * 4 + [hbm] * 5,
        out_specs=(vmem, hbm),
        scratch_shapes=[
            pltpu.VMEM((2, 8, 64, WIDE), BF16),
            pltpu.VMEM((WIDTH, FFS), BF16),
            pltpu.VMEM((WIDTH, FFS), BF16),
            pltpu.VMEM((FFS, WIDTH), BF16),
            pltpu.VMEM((576, 128), BF16),
            pltpu.VMEM((576, 128), BF16),
            pltpu.VMEM((128, KV_RANK), BF16),
            pltpu.VMEM((8, PAD, WIDTH), BF16),
            pltpu.VMEM((8, PAD, WIDTH), BF16),
            pltpu.VMEM((8, PAD, WIDTH), BF16),
            pltpu.VMEM((GROUP, WIDTH), BF16),
            pltpu.VMEM((8, 4, GROUP, 2 * SHARE), BF16),
            pltpu.VMEM((4, 7, GROUP, 2 * SHARE), BF16),
            pltpu.VMEM((4, 8, GROUP, SHARE), BF16),
            pltpu.VMEM((8, PAD, WIDTH), BF16),
            pltpu.VMEM((8, PAD, WIDTH), BF16),
            pltpu.VMEM((8, PAD, WIDTH), BF16),
            pltpu.VMEM((2, 8, 64, WIDTH), F32),
            pltpu.VMEM((2, 8, 64, WIDTH), BF16),
            pltpu.VMEM((2, 8, 64, WIDTH), BF16),
            pltpu.VMEM((3, TOK, WIDTH), BF16),
            pltpu.VMEM((3, TOK, WIDTH), BF16),
            dmas(6), dma, dmas(4), dma, dmas(2, 8, 4), dma, dmas(8),
            dma, dmas(4), dma, dmas(4), dma, dmas(8), dma, dmas(2, 8, 4), dma, dma,
        ],
        compiler_params=pltpu.CompilerParams(
            collective_id=0, has_side_effects=True, vmem_limit_bytes=255 << 18
        ),
        name="moe_attention",
    )(
        x_a, routes.T, route_score.T, lengths.reshape(1, 1), w_gate, w_up, w_down,
        jnp.swapaxes(queries, 1, 2), jnp.swapaxes(cache, 1, 2),
    )


def solution(mesh):
    placed = (
        P(("peer", "sub"), "pool"),
        P(("peer", "sub"), None),
        P(("peer", "sub"), None),
        P("peer", "pool", "sub"),
        P("peer", "pool", "sub"),
        P("peer", "sub", "pool"),
        P(("pool", "peer", "sub"), None, None),
        P(("pool", "peer", "sub"), None, None),
        P(("pool", "peer", "sub")),
    )
    return jax.shard_map(
        per_device,
        mesh=mesh,
        in_specs=placed,
        out_specs=(P(("peer", "sub"), "pool"), P(("pool", "peer", "sub"), None, None)),
        check_vma=False,
    )
```

```python
import functools

import jax
import jax.numpy as jnp
from jax import lax
from jax.experimental import pallas as pl
from jax.experimental.pallas import tpu as pltpu
from jax.sharding import PartitionSpec as P

KV_RANK = 512
SCALE = 192 ** (-0.5)
ROUTED = 2.5
TOK = 16
MOST = 5
WIDTH = 896
WIDE = 1024
FFS = 512
HALF = 8 * MOST
GROUP = 2 * HALF
PAD = 48
SHARE = FFS // 4
MESH = pl.DeviceIdType.MESH
F32, BF16 = jnp.float32, jnp.bfloat16


def kernel(
    x_hbm, routes_hbm, score_hbm, len_ref, wg_hbm, wu_hbm, wd_hbm, q_hbm, c_hbm,
    moe_ref, ctx_hbm,
    routes_ref, score_ref, xb, wg, wu, wd, qv, cv, ctxv, fact, po, pm, pr, sp, rp, hr, yo, ym, ye, co, zs, zr, fs, yr,
    load_sem, y_send, y_recv, ring_send, ring_recv, mate_send, mate_recv,
    rp_send, rp_recv, h_send, h_recv, ym_send, ym_recv, z_send, z_recv, f_send, f_recv,
):
    pool, peer, sub = lax.axis_index("pool"), lax.axis_index("peer"), lax.axis_index("sub")
    row, col = pool // 4, lax.rem(pool, 4)
    up_dev = {"peer": lax.rem(peer + 2, 32)}
    down_dev = {"peer": lax.rem(peer + 30, 32)}
    mate_dev = {"peer": peer + 1 - 2 * lax.rem(peer, 2)}

    def sub_dev(d):
        return {"sub": lax.rem(sub + d, 4)}

    def pool_dev(d):
        return {"pool": lax.rem(pool + d, 8)}

    def send(src, dst, ssem, rsem, dev):
        pltpu.make_async_remote_copy(
            src_ref=src, dst_ref=dst, send_sem=ssem, recv_sem=rsem,
            device_id=dev, device_id_type=MESH,
        ).start()

    def wait(ref, sem):
        pltpu.make_async_copy(ref, ref, sem).wait()

    barrier = pltpu.get_barrier_semaphore()
    partners = [sub_dev(2), sub_dev(1), sub_dev(3), up_dev, down_dev, mate_dev]
    partners += [pool_dev(d) for d in (6, 2, 5, 7, 3, 1, 4)]
    for dev in partners:
        pl.semaphore_signal(barrier, inc=1, device_id=dev, device_id_type=MESH)

    loads = [
        pltpu.make_async_copy(src, dst, load_sem.at[n])
        for n, (src, dst) in enumerate(
            (
                (routes_hbm, routes_ref), (score_hbm, score_ref), (x_hbm, xb.at[0, 0, 0:TOK, 0:WIDTH]),
                (wg_hbm.at[0], wg), (wu_hbm.at[0], wu), (q_hbm.at[0], qv), (c_hbm.at[0], cv), (wd_hbm.at[0], wd),
            )
        )
    ]
    for load in loads:
        load.start()
    loads[0].wait()
    loads[1].wait()

    lane = lax.broadcasted_iota(jnp.int32, (TOK, 128), 1)
    score = score_ref[...]
    weight = ROUTED * score / jnp.sum(score, axis=0, keepdims=True)
    high = weight.astype(BF16)
    eye = lax.broadcasted_iota(jnp.int32, (8, 8), 0) == lax.broadcasted_iota(jnp.int32, (8, 8), 1)
    eye = jnp.where(eye, 1.0, 0.0).astype(BF16)

    def turn(v):
        return lax.dot_general(v, eye, (((0,), (0,)), ((), ())), preferred_element_type=F32)

    names = turn(routes_ref[...].astype(F32).astype(BF16)).astype(jnp.int32)
    low = turn((weight - high.astype(F32)).astype(BF16))
    high = turn(high)
    hit = jnp.zeros((TOK, 128), F32)
    mix = jnp.zeros((TOK, 128), F32)
    for k in range(8):
        expert = names[:, k : k + 1]
        hit = hit + jnp.where(lane == expert, 1.0, 0.0)
        mix = mix + jnp.where(lane == expert + 32, high[:, k : k + 1], 0.0)
        mix = mix + jnp.where(lane == expert + 64, low[:, k : k + 1], 0.0)
    before = (
        lax.broadcasted_iota(jnp.int32, (TOK, TOK), 1) < lax.broadcasted_iota(jnp.int32, (TOK, TOK), 0)
    )
    earlier = jnp.dot(jnp.where(before, 1.0, 0.0).astype(BF16), hit.astype(BF16), preferred_element_type=F32)
    table = (earlier + 1.0) * hit + mix
    xb[0, 0, 0:TOK, WIDTH:WIDE] = table.astype(BF16)

    loads[2].wait()
    pl.semaphore_wait(barrier, len(partners))

    def rows(i):
        return pl.ds(TOK * i, TOK)

    def pass_up(a, i):
        send(xb.at[0, a, rows(i)], xb.at[0, a + 1, rows(i)], ring_send, ring_recv.at[0, a + 1, i], up_dev)

    def pass_down(a, i):
        send(xb.at[1, a, rows(i)], xb.at[1, a + 1, rows(i)], ring_send, ring_recv.at[1, a + 1, i], down_dev)

    for d in (2, 1, 3):
        send(xb.at[0, 0, rows(0)], xb.at[0, 0, rows(4 - d)], y_send, y_recv.at[4 - d], sub_dev(d))
    for i in (0, 1, 3, 2):
        if i:
            wait(xb.at[0, 0, rows(i)], y_recv.at[i])
        pass_up(0, i)
        send(xb.at[0, 0, rows(i)], xb.at[1, 0, rows(i)], ring_send, ring_recv.at[1, 0, i], down_dev)

    ctx_out = pltpu.make_async_copy(ctxv, ctx_hbm.at[0], load_sem.at[8])

    def attention():
        loads[5].wait()
        loads[6].wait()
        entries = cv[...]
        scores = lax.dot_general(qv[...], entries, (((0,), (0,)), ((), ())), preferred_element_type=F32) * SCALE
        valid = lax.broadcasted_iota(jnp.int32, scores.shape, 1) < len_ref[0]
        top = jnp.max(jnp.where(valid, scores, -jnp.inf), axis=1, keepdims=True)
        expo = jnp.where(valid, jnp.exp(scores - top), 0.0)
        probs = (expo / jnp.sum(expo, axis=1, keepdims=True)).astype(BF16)
        ctxv[...] = lax.dot_general(
            probs, entries[0:KV_RANK], (((1,), (1,)), ((), ())), preferred_element_type=F32
        ).astype(BF16)
        ctx_out.start()

    loads[3].wait()
    loads[4].wait()
    loads[7].wait()

    mate = peer + 1 - 2 * lax.rem(peer, 2)
    lanes = lax.broadcasted_iota(jnp.int32, (128, 8), 0)
    wants = lax.broadcasted_iota(jnp.int32, (128, 8), 1)
    expert = jnp.where(lax.rem(wants, 2) == 0, peer, mate)
    slot_of = (wants < 2) & (lanes == expert)
    share_of = (wants >= 2) & (wants < 4) & ((lanes == expert + 32) | (lanes == expert + 64))
    reader = jnp.where(slot_of | share_of, 1.0, 0.0).astype(BF16)
    base = lax.broadcasted_iota(jnp.int32, (128, 1), 0) // TOK * MOST - 1

    def select(k):
        u, h = k // 2, lax.rem(k, 2)
        tab = xb[h, pl.ds(2 * u, 2), :, WIDTH:WIDE].reshape(128, 128)
        facts = jnp.dot(tab, reader, preferred_element_type=F32)
        fact[k] = facts
        slot = facts.astype(jnp.int32)
        mine = jnp.where(slot[:, 0:1] > 0, slot[:, 0:1] + base, -1)
        other = jnp.where(slot[:, 1:2] > 0, slot[:, 1:2] + base + PAD, -1)
        slots = lax.broadcasted_iota(jnp.int32, (128, 128), 1)
        onehot = jnp.where((slots == mine) | (slots == other), 1.0, 0.0).astype(BF16)
        x = xb[h, pl.ds(2 * u, 2), :, 0:WIDTH].reshape(128, WIDTH)
        picked = lax.dot_general(onehot, x, (((0,), (0,)), ((), ())), preferred_element_type=F32).astype(BF16)
        pm[k] = picked[PAD : 2 * PAD]
        send(pm.at[k], pr.at[k], mate_send, mate_recv.at[k], mate_dev)
        po[k] = picked[0:PAD]

    def gates(k):
        u, h = k // 2, lax.rem(k, 2)
        wait(pr.at[k], mate_recv.at[k])
        picked = jnp.concatenate([po[k].astype(F32)[0:HALF], pr[k].astype(F32)[0:HALF]], axis=0).astype(BF16)
        gate = jnp.dot(picked, wg[...], preferred_element_type=F32).astype(BF16)
        for n in range(4):
            sp[k, n, :, 0:SHARE] = gate[:, SHARE * n : SHARE * (n + 1)]
        upper = jnp.dot(picked, wu[...], preferred_element_type=F32).astype(BF16)
        for n in range(4):
            sp[k, n, :, SHARE : 2 * SHARE] = upper[:, SHARE * n : SHARE * (n + 1)]

        def give(d):
            c = lax.rem(col + d, 4)
            dest = h * 4 + c
            place = lax.rem(pool - dest + 8, 8) - 1
            send(sp.at[k, c], rp.at[u, place], rp_send, rp_recv.at[u], {"pool": dest})

        for d in (2, 1, 3):
            give(d)

        @pl.when(h != row)
        def _():
            give(0)

    def hidden(u):
        wait(rp.at[u], rp_recv.at[u])
        total = sp[2 * u + row, col].astype(F32)
        for n in range(7):
            total = total + rp[u, n].astype(F32)
        gate, upper = total[:, 0:SHARE], total[:, SHARE : 2 * SHARE]
        hr[u, pool] = (gate / (1.0 + jnp.exp(-gate)) * upper).astype(BF16)
        for d in (6, 2, 5, 7, 3, 1, 4):
            send(hr.at[u, pool], hr.at[u, pool], h_send, h_recv.at[u], pool_dev(d))

    def down(u):
        wait(hr.at[u, 0:7], h_recv.at[u])
        for h in range(2):
            k = 2 * u + h
            hid = jnp.concatenate([hr[u, 4 * h + n] for n in range(4)], axis=1)
            out = jnp.dot(hid, wd[...], preferred_element_type=F32)
            none = jnp.zeros((PAD - HALF, WIDTH), F32)
            ym[k] = jnp.concatenate([out[HALF:GROUP], none], axis=0).astype(BF16)
            send(ym.at[k], ye.at[k], ym_send, ym_recv.at[k], mate_dev)
            yo[k] = jnp.concatenate([out[0:HALF], none], axis=0).astype(BF16)

    def combine(k):
        u, h = k // 2, lax.rem(k, 2)
        wait(ye.at[k], ym_recv.at[k])
        slots = lax.broadcasted_iota(jnp.int32, (128, PAD), 1)
        facts = fact[k]
        slot = facts.astype(jnp.int32)
        total = None
        for n, part in enumerate((yo, ye)):
            place = jnp.where(slot[:, n : n + 1] > 0, slot[:, n : n + 1] + base, -1)
            onehot = jnp.where(slots == place, 1.0, 0.0).astype(BF16)
            term = facts[:, n + 2 : n + 3] * jnp.dot(onehot, part[k], preferred_element_type=F32)
            total = term if total is None else total + term
        co[h, pl.ds(2 * u, 2)] = total.reshape(2, 64, WIDTH)

    def hop(t, _):
        @pl.when(t <= 8)
        def _():
            for i in (0, 1, 3, 2):
                @pl.when(t <= 7)
                def _():
                    wait(xb.at[0, t, rows(i)], ring_recv.at[0, t, i])

                @pl.when(t <= 6)
                def _():
                    pass_up(t, i)

                wait(xb.at[1, t - 1, rows(i)], ring_recv.at[1, t - 1, i])

                @pl.when(t <= 7)
                def _():
                    pass_down(t - 1, i)

            select(t - 1)

        @pl.when(t >= 2)
        def _():
            gates(t - 2)

        @pl.when((t >= 5) & (lax.rem(t, 2) == 1))
        def _():
            hidden((t - 5) // 2)

        @pl.when((t >= 7) & (lax.rem(t, 2) == 1))
        def _():
            down((t - 7) // 2)

        return 0

    lax.fori_loop(1, 10, hop, 0)
    attention()
    hidden(3)
    down(2)

    def mixes(k, _):
        combine(k)
        return 0

    lax.fori_loop(0, 4, mixes, 0)
    down(3)
    lax.fori_loop(4, 8, mixes, 0)

    def own(h, a, i):
        return co[h, a, rows(i)]

    def back(h, a, i, dev):
        after = lax.rem(a + 7, 8)
        send(zs.at[h, a, rows(i)], zr.at[h, after, rows(i)], z_send, z_recv.at[h, after, i], dev)

    ways = ((0, down_dev), (1, up_dev))
    order = (2, 1, 3, 0)
    for i in order:
        for h, dev in ways:
            zs[h, 7, rows(i)] = own(h, 7, i).astype(BF16)
            back(h, 7, i, dev)

    def home(s, _):
        a = 6 - s
        for i in order:
            for h, dev in ways:
                wait(zr.at[h, a, rows(i)], z_recv.at[h, a, i])
                zs[h, a, rows(i)] = (own(h, a, i) + zr[h, a, rows(i)].astype(F32)).astype(BF16)
                back(h, a, i, dev)
        return 0

    lax.fori_loop(0, 6, home, 0)
    total = None
    for i in order:
        wait(zr.at[1, 0, rows(i)], z_recv.at[1, 0, i])
        zs[1, 0, rows(i)] = (own(1, 0, i) + zr[1, 0, rows(i)].astype(F32)).astype(BF16)
        back(1, 0, i, up_dev)
    for i in order:
        wait(zr.at[0, 0, rows(i)], z_recv.at[0, 0, i])
        wait(zr.at[1, 7, rows(i)], z_recv.at[1, 7, i])
        total = own(0, 0, i) + zr[0, 0, rows(i)].astype(F32) + zr[1, 7, rows(i)].astype(F32)
        if i:
            fs[i - 1] = total.astype(BF16)
            send(fs.at[i - 1], yr.at[i - 1], f_send, f_recv, sub_dev(i))

    ctx_out.wait()
    wait(xb.at[0, 0, 0 : 3 * TOK], y_send)
    wait(xb.at[0, 0:7], ring_send)
    wait(xb.at[1], ring_send)
    wait(pm, mate_send)
    wait(rp, rp_send)
    for u in range(4):
        wait(hr.at[u, 0:7], h_send)
    wait(ym, ym_send)
    wait(zs.at[0, 0:7], z_send)
    wait(zs.at[1], z_send)
    wait(fs, f_send)

    wait(yr, f_recv)
    for n in range(3):
        total = total + yr[n].astype(F32)
    moe_ref[...] = total.astype(BF16)


def keep(v):
    return pltpu.with_memory_space_constraint(v, pltpu.HBM)


def per_device(x_a, routes, route_score, w_gate, w_up, w_down, queries, cache, lengths):
    vmem = pl.BlockSpec(memory_space=pltpu.VMEM)
    hbm = pl.BlockSpec(memory_space=pltpu.HBM)
    dma, dmas = pltpu.SemaphoreType.DMA, lambda *s: pltpu.SemaphoreType.DMA(s)
    return pl.pallas_call(
        kernel,
        out_shape=(
            jax.ShapeDtypeStruct((TOK, WIDTH), BF16),
            jax.ShapeDtypeStruct((1, 128, KV_RANK), BF16),
        ),
        in_specs=[hbm] * 3 + [pl.BlockSpec(memory_space=pltpu.SMEM)] + [hbm] * 5,
        out_specs=(vmem, pl.BlockSpec(memory_space=pl.ANY)),
        scratch_shapes=[
            pltpu.VMEM((8, TOK), jnp.int32),
            pltpu.VMEM((8, TOK), F32),
            pltpu.VMEM((2, 8, 64, WIDE), BF16),
            pltpu.VMEM((WIDTH, FFS), BF16),
            pltpu.VMEM((WIDTH, FFS), BF16),
            pltpu.VMEM((FFS, WIDTH), BF16),
            pltpu.VMEM((576, 128), BF16),
            pltpu.VMEM((576, 128), BF16),
            pltpu.VMEM((128, KV_RANK), BF16),
            pltpu.VMEM((8, 128, 8), F32),
            pltpu.VMEM((8, PAD, WIDTH), BF16),
            pltpu.VMEM((8, PAD, WIDTH), BF16),
            pltpu.VMEM((8, PAD, WIDTH), BF16),
            pltpu.VMEM((8, 4, GROUP, 2 * SHARE), BF16),
            pltpu.VMEM((4, 7, GROUP, 2 * SHARE), BF16),
            pltpu.VMEM((4, 8, GROUP, SHARE), BF16),
            pltpu.VMEM((8, PAD, WIDTH), BF16),
            pltpu.VMEM((8, PAD, WIDTH), BF16),
            pltpu.VMEM((8, PAD, WIDTH), BF16),
            pltpu.VMEM((2, 8, 64, WIDTH), F32),
            pltpu.VMEM((2, 8, 64, WIDTH), BF16),
            pltpu.VMEM((2, 8, 64, WIDTH), BF16),
            pltpu.VMEM((3, TOK, WIDTH), BF16),
            pltpu.VMEM((3, TOK, WIDTH), BF16),
            dmas(9), dma, dmas(4), dma, dmas(2, 8, 4), dma, dmas(8),
            dma, dmas(4), dma, dmas(4), dma, dmas(8), dma, dmas(2, 8, 4), dma, dma,
        ],
        compiler_params=pltpu.CompilerParams(
            collective_id=0, has_side_effects=True, vmem_limit_bytes=48 << 20
        ),
        name="moe_attention",
    )(
        keep(x_a), keep(routes.T), keep(route_score.T), lengths, keep(w_gate), keep(w_up), keep(w_down),
        keep(jnp.swapaxes(queries, 1, 2)), keep(jnp.swapaxes(cache, 1, 2)),
    )


def solution(mesh):
    placed = (
        P(("peer", "sub"), "pool"),
        P(("peer", "sub"), None),
        P(("peer", "sub"), None),
        P("peer", "pool", "sub"),
        P("peer", "pool", "sub"),
        P("peer", "sub", "pool"),
        P(("pool", "peer", "sub"), None, None),
        P(("pool", "peer", "sub"), None, None),
        P(("pool", "peer", "sub")),
    )
    return jax.shard_map(
        per_device,
        mesh=mesh,
        in_specs=placed,
        out_specs=(P(("peer", "sub"), "pool"), P(("pool", "peer", "sub"), None, None)),
        check_vma=False,
    )
```

```python
import functools

import jax
import jax.numpy as jnp
from jax import lax
from jax.experimental import pallas as pl
from jax.experimental.pallas import tpu as pltpu
from jax.sharding import PartitionSpec as P

KV_RANK = 512
SCALE = 192 ** (-0.5)
ROUTED = 2.5
TOK = 16
MOST = 5
WIDTH = 896
WIDE = 1024
FFS = 512
HALF = 8 * MOST
GROUP = 2 * HALF
PAD = 48
SHARE = FFS // 4
MESH = pl.DeviceIdType.MESH
F32, BF16 = jnp.float32, jnp.bfloat16


def kernel(
    x_hbm, routes_hbm, score_hbm, len_ref, wg_hbm, wu_hbm, wd_hbm, q_hbm, c_hbm,
    moe_ref, ctx_hbm,
    routes_ref, score_ref, xb, wg, wu, wd, qv, cv, ctxv, fact, po, pm, pr, sp, rp, hr, yo, ym, ye, co, zs, zr, fs, yr,
    load_sem, y_send, y_recv, ring_send, ring_recv, mate_send, mate_recv,
    rp_send, rp_recv, h_send, h_recv, ym_send, ym_recv, z_send, z_recv, f_send, f_recv,
):
    pool, peer, sub = lax.axis_index("pool"), lax.axis_index("peer"), lax.axis_index("sub")
    row, col = pool // 4, lax.rem(pool, 4)
    up_dev = {"peer": lax.rem(peer + 2, 32)}
    down_dev = {"peer": lax.rem(peer + 30, 32)}
    mate_dev = {"peer": peer + 1 - 2 * lax.rem(peer, 2)}

    def sub_dev(d):
        return {"sub": lax.rem(sub + d, 4)}

    def pool_dev(d):
        return {"pool": lax.rem(pool + d, 8)}

    def send(src, dst, ssem, rsem, dev):
        pltpu.make_async_remote_copy(
            src_ref=src, dst_ref=dst, send_sem=ssem, recv_sem=rsem,
            device_id=dev, device_id_type=MESH,
        ).start()

    def wait(ref, sem):
        pltpu.make_async_copy(ref, ref, sem).wait()

    loads = [
        pltpu.make_async_copy(src, dst, load_sem.at[n])
        for n, (src, dst) in enumerate(
            (
                (routes_hbm, routes_ref), (score_hbm, score_ref), (x_hbm, xb.at[0, 0, 0:TOK, 0:WIDTH]),
                (wg_hbm.at[0], wg), (wu_hbm.at[0], wu), (q_hbm.at[0], qv), (c_hbm.at[0], cv), (wd_hbm.at[0], wd),
            )
        )
    ]
    for load in loads[:3]:
        load.start()

    barrier = pltpu.get_barrier_semaphore()
    partners = [sub_dev(2), sub_dev(1), sub_dev(3), up_dev, down_dev, mate_dev]
    partners += [pool_dev(d) for d in (6, 2, 5, 7, 3, 1, 4)]
    for dev in partners:
        pl.semaphore_signal(barrier, inc=1, device_id=dev, device_id_type=MESH)

    for load in loads[3:]:
        load.start()
    loads[0].wait()
    loads[1].wait()

    lane = lax.broadcasted_iota(jnp.int32, (TOK, 128), 1)
    score = score_ref[...]
    weight = ROUTED * score / jnp.sum(score, axis=0, keepdims=True)
    high = weight.astype(BF16)
    eye = lax.broadcasted_iota(jnp.int32, (8, 8), 0) == lax.broadcasted_iota(jnp.int32, (8, 8), 1)
    eye = jnp.where(eye, 1.0, 0.0).astype(BF16)

    def turn(v):
        return lax.dot_general(v, eye, (((0,), (0,)), ((), ())), preferred_element_type=F32)

    names = turn(routes_ref[...].astype(F32).astype(BF16)).astype(jnp.int32)
    low = turn((weight - high.astype(F32)).astype(BF16))
    high = turn(high)
    hit = jnp.zeros((TOK, 128), F32)
    mix = jnp.zeros((TOK, 128), F32)
    for k in range(8):
        expert = names[:, k : k + 1]
        hit = hit + jnp.where(lane == expert, 1.0, 0.0)
        mix = mix + jnp.where(lane == expert + 32, high[:, k : k + 1], 0.0)
        mix = mix + jnp.where(lane == expert + 64, low[:, k : k + 1], 0.0)
    before = (
        lax.broadcasted_iota(jnp.int32, (TOK, TOK), 1) < lax.broadcasted_iota(jnp.int32, (TOK, TOK), 0)
    )
    earlier = jnp.dot(jnp.where(before, 1.0, 0.0).astype(BF16), hit.astype(BF16), preferred_element_type=F32)
    table = (earlier + 1.0) * hit + mix
    xb[0, 0, 0:TOK, WIDTH:WIDE] = table.astype(BF16)

    loads[2].wait()
    pl.semaphore_wait(barrier, len(partners))

    def rows(i):
        return pl.ds(TOK * i, TOK)

    def pass_up(a, i):
        send(xb.at[0, a, rows(i)], xb.at[0, a + 1, rows(i)], ring_send, ring_recv.at[0, a + 1, i], up_dev)

    def pass_down(a, i):
        send(xb.at[1, a, rows(i)], xb.at[1, a + 1, rows(i)], ring_send, ring_recv.at[1, a + 1, i], down_dev)

    for d in (2, 1, 3):
        send(xb.at[0, 0, rows(0)], xb.at[0, 0, rows(4 - d)], y_send, y_recv.at[4 - d], sub_dev(d))
    for i in (0, 1, 3, 2):
        if i:
            wait(xb.at[0, 0, rows(i)], y_recv.at[i])
        pass_up(0, i)
        send(xb.at[0, 0, rows(i)], xb.at[1, 0, rows(i)], ring_send, ring_recv.at[1, 0, i], down_dev)

    ctx_out = pltpu.make_async_copy(ctxv, ctx_hbm.at[0], load_sem.at[8])

    def attention():
        loads[5].wait()
        loads[6].wait()
        entries = cv[...]
        scores = lax.dot_general(qv[...], entries, (((0,), (0,)), ((), ())), preferred_element_type=F32) * SCALE
        valid = lax.broadcasted_iota(jnp.int32, scores.shape, 1) < len_ref[0]
        top = jnp.max(jnp.where(valid, scores, -jnp.inf), axis=1, keepdims=True)
        expo = jnp.where(valid, jnp.exp(scores - top), 0.0)
        probs = (expo / jnp.sum(expo, axis=1, keepdims=True)).astype(BF16)
        ctxv[...] = lax.dot_general(
            probs, entries[0:KV_RANK], (((1,), (1,)), ((), ())), preferred_element_type=F32
        ).astype(BF16)
        ctx_out.start()

    loads[3].wait()
    loads[4].wait()
    loads[7].wait()

    mate = peer + 1 - 2 * lax.rem(peer, 2)
    lanes = lax.broadcasted_iota(jnp.int32, (128, 8), 0)
    wants = lax.broadcasted_iota(jnp.int32, (128, 8), 1)
    expert = jnp.where(lax.rem(wants, 2) == 0, peer, mate)
    slot_of = (wants < 2) & (lanes == expert)
    share_of = (wants >= 2) & (wants < 4) & ((lanes == expert + 32) | (lanes == expert + 64))
    reader = jnp.where(slot_of | share_of, 1.0, 0.0).astype(BF16)
    base = lax.broadcasted_iota(jnp.int32, (128, 1), 0) // TOK * MOST - 1

    def select(k):
        u, h = k // 2, lax.rem(k, 2)
        tab = xb[h, pl.ds(2 * u, 2), :, WIDTH:WIDE].reshape(128, 128)
        facts = jnp.dot(tab, reader, preferred_element_type=F32)
        fact[k] = facts
        slot = facts.astype(jnp.int32)
        mine = jnp.where(slot[:, 0:1] > 0, slot[:, 0:1] + base, -1)
        other = jnp.where(slot[:, 1:2] > 0, slot[:, 1:2] + base + PAD, -1)
        slots = lax.broadcasted_iota(jnp.int32, (128, 128), 1)
        onehot = jnp.where((slots == mine) | (slots == other), 1.0, 0.0).astype(BF16)
        x = xb[h, pl.ds(2 * u, 2), :, 0:WIDTH].reshape(128, WIDTH)
        picked = lax.dot_general(onehot, x, (((0,), (0,)), ((), ())), preferred_element_type=F32).astype(BF16)
        pm[k] = picked[PAD : 2 * PAD]
        send(pm.at[k], pr.at[k], mate_send, mate_recv.at[k], mate_dev)
        po[k] = picked[0:PAD]

    def gates(k):
        u, h = k // 2, lax.rem(k, 2)
        wait(pr.at[k], mate_recv.at[k])
        picked = jnp.concatenate([po[k].astype(F32)[0:HALF], pr[k].astype(F32)[0:HALF]], axis=0).astype(BF16)
        gate = jnp.dot(picked, wg[...], preferred_element_type=F32).astype(BF16)
        for n in range(4):
            sp[k, n, :, 0:SHARE] = gate[:, SHARE * n : SHARE * (n + 1)]
        upper = jnp.dot(picked, wu[...], preferred_element_type=F32).astype(BF16)
        for n in range(4):
            sp[k, n, :, SHARE : 2 * SHARE] = upper[:, SHARE * n : SHARE * (n + 1)]

        def give(d):
            c = lax.rem(col + d, 4)
            dest = h * 4 + c
            place = lax.rem(pool - dest + 8, 8) - 1
            send(sp.at[k, c], rp.at[u, place], rp_send, rp_recv.at[u], {"pool": dest})

        for d in (2, 1, 3):
            give(d)

        @pl.when(h != row)
        def _():
            give(0)

    def hidden(u):
        wait(rp.at[u], rp_recv.at[u])
        total = sp[2 * u + row, col].astype(F32)
        for n in range(7):
            total = total + rp[u, n].astype(F32)
        gate, upper = total[:, 0:SHARE], total[:, SHARE : 2 * SHARE]
        hr[u, pool] = (gate / (1.0 + jnp.exp(-gate)) * upper).astype(BF16)
        for d in (6, 2, 5, 7, 3, 1, 4):
            send(hr.at[u, pool], hr.at[u, pool], h_send, h_recv.at[u, row], pool_dev(d))

    def down(k):
        u, h = k // 2, lax.rem(k, 2)

        @pl.when(row == h)
        def _():
            wait(hr.at[u, 0:3], h_recv.at[u, h])

        @pl.when(row != h)
        def _():
            wait(hr.at[u, 0:4], h_recv.at[u, h])

        hid = jnp.concatenate([hr[u, 4 * h + n] for n in range(4)], axis=1)
        out = jnp.dot(hid, wd[...], preferred_element_type=F32)
        none = jnp.zeros((PAD - HALF, WIDTH), F32)
        ym[k] = jnp.concatenate([out[HALF:GROUP], none], axis=0).astype(BF16)
        send(ym.at[k], ye.at[k], ym_send, ym_recv.at[k], mate_dev)
        yo[k] = jnp.concatenate([out[0:HALF], none], axis=0).astype(BF16)

    def combine(k):
        u, h = k // 2, lax.rem(k, 2)
        wait(ye.at[k], ym_recv.at[k])
        slots = lax.broadcasted_iota(jnp.int32, (128, PAD), 1)
        facts = fact[k]
        slot = facts.astype(jnp.int32)
        total = None
        for n, part in enumerate((yo, ye)):
            place = jnp.where(slot[:, n : n + 1] > 0, slot[:, n : n + 1] + base, -1)
            onehot = jnp.where(slots == place, 1.0, 0.0).astype(BF16)
            term = facts[:, n + 2 : n + 3] * jnp.dot(onehot, part[k], preferred_element_type=F32)
            total = term if total is None else total + term
        co[h, pl.ds(2 * u, 2)] = total.reshape(2, 64, WIDTH)

    def hop(t, _):
        @pl.when(t <= 8)
        def _():
            for i in (0, 1, 3, 2):
                @pl.when(t <= 7)
                def _():
                    wait(xb.at[0, t, rows(i)], ring_recv.at[0, t, i])

                @pl.when(t <= 6)
                def _():
                    pass_up(t, i)

                wait(xb.at[1, t - 1, rows(i)], ring_recv.at[1, t - 1, i])

                @pl.when(t <= 7)
                def _():
                    pass_down(t - 1, i)

            select(t - 1)

        @pl.when(t >= 2)
        def _():
            gates(t - 2)

        @pl.when((t >= 5) & (lax.rem(t, 2) == 1))
        def _():
            hidden((t - 5) // 2)

        @pl.when((t >= 7) & (lax.rem(t, 2) == 1))
        def _():
            down(t - 7)
            down(t - 6)

        return 0

    lax.fori_loop(1, 10, hop, 0)
    attention()
    hidden(3)

    def mixes(k, _):
        combine(k)
        return 0

    def downs(k, _):
        down(k)
        return 0

    lax.fori_loop(4, 6, downs, 0)
    lax.fori_loop(0, 4, mixes, 0)
    down(6)
    lax.fori_loop(4, 6, mixes, 0)
    down(7)
    lax.fori_loop(6, 8, mixes, 0)

    runs = (pl.ds(0, 512), pl.ds(512, WIDTH - 512))

    def back(h, a, i, f, dev):
        after = lax.rem(a + 7, 8)
        send(
            zs.at[h, a, rows(i), runs[f]], zr.at[h, after, rows(i), runs[f]],
            z_send, z_recv.at[h, after, 2 * i + f], dev,
        )

    def arrive(h, a, i, f):
        wait(zr.at[h, a, rows(i), runs[f]], z_recv.at[h, a, 2 * i + f])

    def onward(h, a, i, f, dev):
        arrive(h, a, i, f)
        mine, theirs = co[h, a, rows(i), runs[f]], zr[h, a, rows(i), runs[f]]
        zs[h, a, rows(i), runs[f]] = (mine + theirs.astype(F32)).astype(BF16)
        back(h, a, i, f, dev)

    ways = ((1, up_dev), (0, down_dev))
    order = (2, 1, 3, 0)
    for i in order:
        for f in range(2):
            for h, dev in ways:
                zs[h, 7, rows(i), runs[f]] = co[h, 7, rows(i), runs[f]].astype(BF16)
                back(h, 7, i, f, dev)

    def home(s, _):
        for i in order:
            for f in range(2):
                for h, dev in ways:
                    onward(h, 6 - s, i, f, dev)
        return 0

    lax.fori_loop(0, 6, home, 0)
    total = None
    for i in order:
        for f in range(2):
            onward(1, 0, i, f, up_dev)
    for i in order:
        for f in range(2):
            arrive(0, 0, i, f)
            arrive(1, 7, i, f)
        total = co[0, 0, rows(i)] + zr[0, 0, rows(i)].astype(F32) + zr[1, 7, rows(i)].astype(F32)
        if i:
            fs[i - 1] = total.astype(BF16)
            send(fs.at[i - 1], yr.at[i - 1], f_send, f_recv, sub_dev(i))

    ctx_out.wait()
    wait(xb.at[0, 0, 0 : 3 * TOK], y_send)
    wait(xb.at[0, 0:7], ring_send)
    wait(xb.at[1], ring_send)
    wait(pm, mate_send)
    wait(rp, rp_send)
    for u in range(4):
        wait(hr.at[u, 0:7], h_send)
    wait(ym, ym_send)
    wait(zs.at[0, 0:7], z_send)
    wait(zs.at[1], z_send)
    wait(fs, f_send)

    wait(yr, f_recv)
    for n in range(3):
        total = total + yr[n].astype(F32)
    moe_ref[...] = total.astype(BF16)


def keep(v):
    return pltpu.with_memory_space_constraint(v, pltpu.HBM)


def per_device(x_a, routes, route_score, w_gate, w_up, w_down, queries, cache, lengths):
    vmem = pl.BlockSpec(memory_space=pltpu.VMEM)
    hbm = pl.BlockSpec(memory_space=pltpu.HBM)
    dma, dmas = pltpu.SemaphoreType.DMA, lambda *s: pltpu.SemaphoreType.DMA(s)
    return pl.pallas_call(
        kernel,
        out_shape=(
            jax.ShapeDtypeStruct((TOK, WIDTH), BF16),
            jax.ShapeDtypeStruct((1, 128, KV_RANK), BF16),
        ),
        in_specs=[hbm] * 3 + [pl.BlockSpec(memory_space=pltpu.SMEM)] + [hbm] * 5,
        out_specs=(vmem, pl.BlockSpec(memory_space=pl.ANY)),
        scratch_shapes=[
            pltpu.VMEM((8, TOK), jnp.int32),
            pltpu.VMEM((8, TOK), F32),
            pltpu.VMEM((2, 8, 64, WIDE), BF16),
            pltpu.VMEM((WIDTH, FFS), BF16),
            pltpu.VMEM((WIDTH, FFS), BF16),
            pltpu.VMEM((FFS, WIDTH), BF16),
            pltpu.VMEM((576, 128), BF16),
            pltpu.VMEM((576, 128), BF16),
            pltpu.VMEM((128, KV_RANK), BF16),
            pltpu.VMEM((8, 128, 8), F32),
            pltpu.VMEM((8, PAD, WIDTH), BF16),
            pltpu.VMEM((8, PAD, WIDTH), BF16),
            pltpu.VMEM((8, PAD, WIDTH), BF16),
            pltpu.VMEM((8, 4, GROUP, 2 * SHARE), BF16),
            pltpu.VMEM((4, 7, GROUP, 2 * SHARE), BF16),
            pltpu.VMEM((4, 8, GROUP, SHARE), BF16),
            pltpu.VMEM((8, PAD, WIDTH), BF16),
            pltpu.VMEM((8, PAD, WIDTH), BF16),
            pltpu.VMEM((8, PAD, WIDTH), BF16),
            pltpu.VMEM((2, 8, 64, WIDTH), F32),
            pltpu.VMEM((2, 8, 64, WIDTH), BF16),
            pltpu.VMEM((2, 8, 64, WIDTH), BF16),
            pltpu.VMEM((3, TOK, WIDTH), BF16),
            pltpu.VMEM((3, TOK, WIDTH), BF16),
            dmas(9), dma, dmas(4), dma, dmas(2, 8, 4), dma, dmas(8),
            dma, dmas(4), dma, dmas(4, 2), dma, dmas(8), dma, dmas(2, 8, 8), dma, dma,
        ],
        compiler_params=pltpu.CompilerParams(
            collective_id=0, has_side_effects=True, vmem_limit_bytes=48 << 20
        ),
        name="moe_attention",
    )(
        keep(x_a), keep(routes.T), keep(route_score.T), lengths, keep(w_gate), keep(w_up), keep(w_down),
        keep(jnp.swapaxes(queries, 1, 2)), keep(jnp.swapaxes(cache, 1, 2)),
    )


def solution(mesh):
    placed = (
        P(("peer", "sub"), "pool"),
        P(("peer", "sub"), None),
        P(("peer", "sub"), None),
        P("peer", "pool", "sub"),
        P("peer", "pool", "sub"),
        P("peer", "sub", "pool"),
        P(("pool", "peer", "sub"), None, None),
        P(("pool", "peer", "sub"), None, None),
        P(("pool", "peer", "sub")),
    )
    return jax.shard_map(
        per_device,
        mesh=mesh,
        in_specs=placed,
        out_specs=(P(("peer", "sub"), "pool"), P(("pool", "peer", "sub"), None, None)),
        check_vma=False,
    )
```

```python
import functools

import jax
import jax.numpy as jnp
from jax import lax
from jax.experimental import pallas as pl
from jax.experimental.pallas import tpu as pltpu
from jax.sharding import PartitionSpec as P

KV_RANK = 512
SCALE = 192 ** (-0.5)
ROUTED = 2.5
TOK = 16
MOST = 5
WIDTH = 896
WIDE = 1024
FFS = 512
HALF = 8 * MOST
GROUP = 2 * HALF
PAD = 48
SHARE = FFS // 4
MESH = pl.DeviceIdType.MESH
F32, BF16 = jnp.float32, jnp.bfloat16


def kernel(
    x_hbm, routes_hbm, score_hbm, len_ref, wg_hbm, wu_hbm, wd_hbm, q_hbm, c_hbm,
    moe_ref, ctx_hbm,
    routes_ref, score_ref, xb, wg, wu, wd, qv, cv, ctxv, fact, po, pm, pr, sp, rp, hr, yo, ym, ye, co, zs, zr, fs, yr,
    load_sem, y_send, y_recv, ring_send, ring_recv, mate_send, mate_recv,
    rp_send, rp_recv, h_send, h_recv, ym_send, ym_recv, z_send, z_recv, f_send, f_recv,
):
    pool, peer, sub = lax.axis_index("pool"), lax.axis_index("peer"), lax.axis_index("sub")
    row, col = pool // 4, lax.rem(pool, 4)
    up_dev = {"peer": lax.rem(peer + 2, 32)}
    down_dev = {"peer": lax.rem(peer + 30, 32)}
    mate_dev = {"peer": peer + 1 - 2 * lax.rem(peer, 2)}

    def sub_dev(d):
        return {"sub": lax.rem(sub + d, 4)}

    def pool_dev(d):
        return {"pool": lax.rem(pool + d, 8)}

    def send(src, dst, ssem, rsem, dev):
        pltpu.make_async_remote_copy(
            src_ref=src, dst_ref=dst, send_sem=ssem, recv_sem=rsem,
            device_id=dev, device_id_type=MESH,
        ).start()

    def wait(ref, sem):
        pltpu.make_async_copy(ref, ref, sem).wait()

    loads = [
        pltpu.make_async_copy(src, dst, load_sem.at[n])
        for n, (src, dst) in enumerate(
            (
                (routes_hbm, routes_ref), (score_hbm, score_ref), (x_hbm, xb.at[0, 0, 0:TOK, 0:WIDTH]),
                (wg_hbm.at[0], wg), (wu_hbm.at[0], wu), (q_hbm.at[0], qv), (c_hbm.at[0], cv), (wd_hbm.at[0], wd),
            )
        )
    ]
    for load in loads[:3]:
        load.start()

    barrier = pltpu.get_barrier_semaphore()
    partners = [sub_dev(2), sub_dev(1), sub_dev(3), up_dev, down_dev, mate_dev]
    partners += [pool_dev(d) for d in (6, 2, 5, 7, 3, 1, 4)]
    for dev in partners:
        pl.semaphore_signal(barrier, inc=1, device_id=dev, device_id_type=MESH)

    for load in loads[3:]:
        load.start()
    loads[0].wait()
    loads[1].wait()

    lane = lax.broadcasted_iota(jnp.int32, (TOK, 128), 1)
    score = score_ref[...]
    weight = ROUTED * score / jnp.sum(score, axis=0, keepdims=True)
    high = weight.astype(BF16)
    eye = lax.broadcasted_iota(jnp.int32, (8, 8), 0) == lax.broadcasted_iota(jnp.int32, (8, 8), 1)
    eye = jnp.where(eye, 1.0, 0.0).astype(BF16)

    def turn(v):
        return lax.dot_general(v, eye, (((0,), (0,)), ((), ())), preferred_element_type=F32)

    names = turn(routes_ref[...].astype(F32).astype(BF16)).astype(jnp.int32)
    low = turn((weight - high.astype(F32)).astype(BF16))
    high = turn(high)
    hit = jnp.zeros((TOK, 128), F32)
    mix = jnp.zeros((TOK, 128), F32)
    for k in range(8):
        expert = names[:, k : k + 1]
        hit = hit + jnp.where(lane == expert, 1.0, 0.0)
        mix = mix + jnp.where(lane == expert + 32, high[:, k : k + 1], 0.0)
        mix = mix + jnp.where(lane == expert + 64, low[:, k : k + 1], 0.0)
    before = (
        lax.broadcasted_iota(jnp.int32, (TOK, TOK), 1) < lax.broadcasted_iota(jnp.int32, (TOK, TOK), 0)
    )
    earlier = jnp.dot(jnp.where(before, 1.0, 0.0).astype(BF16), hit.astype(BF16), preferred_element_type=F32)
    table = (earlier + 1.0) * hit + mix
    xb[0, 0, 0:TOK, WIDTH:WIDE] = table.astype(BF16)

    loads[2].wait()
    pl.semaphore_wait(barrier, len(partners))

    def rows(i):
        return pl.ds(TOK * i, TOK)

    def pass_up(a, i):
        send(xb.at[0, a, rows(i)], xb.at[0, a + 1, rows(i)], ring_send, ring_recv.at[0, a + 1, i], up_dev)

    def pass_down(a, i):
        send(xb.at[1, a, rows(i)], xb.at[1, a + 1, rows(i)], ring_send, ring_recv.at[1, a + 1, i], down_dev)

    for d in (2, 1, 3):
        send(xb.at[0, 0, rows(0)], xb.at[0, 0, rows(4 - d)], y_send, y_recv.at[4 - d], sub_dev(d))
    for i in (0, 1, 3, 2):
        if i:
            wait(xb.at[0, 0, rows(i)], y_recv.at[i])
        pass_up(0, i)
        send(xb.at[0, 0, rows(i)], xb.at[1, 0, rows(i)], ring_send, ring_recv.at[1, 0, i], down_dev)

    ctx_out = pltpu.make_async_copy(ctxv, ctx_hbm.at[0], load_sem.at[8])

    def attention():
        loads[5].wait()
        loads[6].wait()
        entries = cv[...]
        scores = lax.dot_general(qv[...], entries, (((0,), (0,)), ((), ())), preferred_element_type=F32) * SCALE
        valid = lax.broadcasted_iota(jnp.int32, scores.shape, 1) < len_ref[0]
        top = jnp.max(jnp.where(valid, scores, -jnp.inf), axis=1, keepdims=True)
        expo = jnp.where(valid, jnp.exp(scores - top), 0.0)
        probs = (expo / jnp.sum(expo, axis=1, keepdims=True)).astype(BF16)
        ctxv[...] = lax.dot_general(
            probs, entries[0:KV_RANK], (((1,), (1,)), ((), ())), preferred_element_type=F32
        ).astype(BF16)
        ctx_out.start()

    loads[3].wait()
    loads[4].wait()
    loads[7].wait()

    mate = peer + 1 - 2 * lax.rem(peer, 2)
    lanes = lax.broadcasted_iota(jnp.int32, (128, 8), 0)
    wants = lax.broadcasted_iota(jnp.int32, (128, 8), 1)
    expert = jnp.where(lax.rem(wants, 2) == 0, peer, mate)
    slot_of = (wants < 2) & (lanes == expert)
    share_of = (wants >= 2) & (wants < 4) & ((lanes == expert + 32) | (lanes == expert + 64))
    reader = jnp.where(slot_of | share_of, 1.0, 0.0).astype(BF16)
    base = lax.broadcasted_iota(jnp.int32, (128, 1), 0) // TOK * MOST - 1

    def select(k):
        u, h = k // 2, k - k // 2 * 2
        tab = xb[h, pl.ds(2 * u, 2), :, WIDTH:WIDE].reshape(128, 128)
        facts = jnp.dot(tab, reader, preferred_element_type=F32)
        fact[k] = facts
        slot = facts.astype(jnp.int32)
        mine = jnp.where(slot[:, 0:1] > 0, slot[:, 0:1] + base, -1)
        other = jnp.where(slot[:, 1:2] > 0, slot[:, 1:2] + base + PAD, -1)
        slots = lax.broadcasted_iota(jnp.int32, (128, 128), 1)
        onehot = jnp.where((slots == mine) | (slots == other), 1.0, 0.0).astype(BF16)
        x = xb[h, pl.ds(2 * u, 2), :, 0:WIDTH].reshape(128, WIDTH)
        picked = lax.dot_general(onehot, x, (((0,), (0,)), ((), ())), preferred_element_type=F32).astype(BF16)
        pm[k] = picked[PAD : 2 * PAD]
        send(pm.at[k], pr.at[k], mate_send, mate_recv.at[k], mate_dev)
        po[k] = picked[0:PAD]

    def gates(k):
        u, h = k // 2, k - k // 2 * 2
        wait(pr.at[k], mate_recv.at[k])
        picked = jnp.concatenate([po[k].astype(F32)[0:HALF], pr[k].astype(F32)[0:HALF]], axis=0).astype(BF16)
        gate = jnp.dot(picked, wg[...], preferred_element_type=F32).astype(BF16)
        for n in range(4):
            sp[k, n, :, 0:SHARE] = gate[:, SHARE * n : SHARE * (n + 1)]
        upper = jnp.dot(picked, wu[...], preferred_element_type=F32).astype(BF16)
        for n in range(4):
            sp[k, n, :, SHARE : 2 * SHARE] = upper[:, SHARE * n : SHARE * (n + 1)]

        def give(d):
            c = lax.rem(col + d, 4)
            dest = h * 4 + c
            place = lax.rem(pool - dest + 8, 8) - 1
            send(sp.at[k, c], rp.at[u, place], rp_send, rp_recv.at[u], {"pool": dest})

        for d in (2, 1, 3):
            give(d)

        @pl.when(row != h)
        def _():
            give(0)

    def hidden(u):
        wait(rp.at[u], rp_recv.at[u])
        total = sp[2 * u + row, col].astype(F32)
        for n in range(7):
            total = total + rp[u, n].astype(F32)
        gate, upper = total[:, 0:SHARE], total[:, SHARE : 2 * SHARE]
        hr[u, pool] = (gate / (1.0 + jnp.exp(-gate)) * upper).astype(BF16)
        for d in (6, 2, 5, 7, 3, 1, 4):
            send(hr.at[u, pool], hr.at[u, pool], h_send, h_recv.at[u, row], pool_dev(d))

    def down(k):
        u, h = k // 2, k - k // 2 * 2

        @pl.when(row == h)
        def _():
            wait(hr.at[u, 0:3], h_recv.at[u, h])

        @pl.when(row != h)
        def _():
            wait(hr.at[u, 0:4], h_recv.at[u, h])

        hid = jnp.concatenate([hr[u, 4 * h + n] for n in range(4)], axis=1)
        out = jnp.dot(hid, wd[...], preferred_element_type=F32)
        none = jnp.zeros((PAD - HALF, WIDTH), F32)
        ym[k] = jnp.concatenate([out[HALF:GROUP], none], axis=0).astype(BF16)
        send(ym.at[k], ye.at[k], ym_send, ym_recv.at[k], mate_dev)
        yo[k] = jnp.concatenate([out[0:HALF], none], axis=0).astype(BF16)

    def combine(k):
        u, h = k // 2, k - k // 2 * 2
        wait(ye.at[k], ym_recv.at[k])
        slots = lax.broadcasted_iota(jnp.int32, (128, PAD), 1)
        facts = fact[k]
        slot = facts.astype(jnp.int32)
        total = None
        for n, part in enumerate((yo, ye)):
            place = jnp.where(slot[:, n : n + 1] > 0, slot[:, n : n + 1] + base, -1)
            onehot = jnp.where(slots == place, 1.0, 0.0).astype(BF16)
            term = facts[:, n + 2 : n + 3] * jnp.dot(onehot, part[k], preferred_element_type=F32)
            total = term if total is None else total + term
        co[h, pl.ds(2 * u, 2)] = total.reshape(2, 64, WIDTH)

    def hop(t, _):
        looped = not isinstance(t, int)
        for i in (0, 1, 3, 2):
            if looped or t <= 7:
                wait(xb.at[0, t, rows(i)], ring_recv.at[0, t, i])
            if looped:
                pass_up(t, i)
            wait(xb.at[1, t - 1, rows(i)], ring_recv.at[1, t - 1, i])
            if looped or t <= 7:
                pass_down(t - 1, i)
        select(t - 1)
        if not looped:
            gates(t - 2)
            return 0

        @pl.when(t >= 2)
        def _():
            gates(t - 2)

        @pl.when(t == 5)
        def _():
            hidden(0)

        return 0

    lax.fori_loop(1, 7, hop, 0)
    hop(7, 0)
    hidden(1)
    down(0)
    down(1)
    hop(8, 0)
    gates(7)
    hidden(2)
    down(2)
    down(3)
    attention()
    hidden(3)

    def mixes(k, _):
        combine(k)
        return 0

    def downs(k, _):
        down(k)
        return 0

    lax.fori_loop(4, 6, downs, 0)
    lax.fori_loop(0, 4, mixes, 0)
    down(6)
    lax.fori_loop(4, 6, mixes, 0)
    down(7)
    lax.fori_loop(6, 8, mixes, 0)

    runs = (pl.ds(0, 512), pl.ds(512, WIDTH - 512))

    def back(h, a, i, f, dev):
        after = lax.rem(a + 7, 8)
        send(
            zs.at[h, a, rows(i), runs[f]], zr.at[h, after, rows(i), runs[f]],
            z_send, z_recv.at[h, after, 2 * i + f], dev,
        )

    def arrive(h, a, i, f):
        wait(zr.at[h, a, rows(i), runs[f]], z_recv.at[h, a, 2 * i + f])

    def onward(h, a, i, f, dev):
        arrive(h, a, i, f)
        mine, theirs = co[h, a, rows(i), runs[f]], zr[h, a, rows(i), runs[f]]
        zs[h, a, rows(i), runs[f]] = (mine + theirs.astype(F32)).astype(BF16)
        back(h, a, i, f, dev)

    ways = ((1, up_dev), (0, down_dev))
    order = (2, 1, 3, 0)
    for i in order:
        for f in range(2):
            for h, dev in ways:
                zs[h, 7, rows(i), runs[f]] = co[h, 7, rows(i), runs[f]].astype(BF16)
                back(h, 7, i, f, dev)

    def home(s, _):
        for i in order:
            for f in range(2):
                for h, dev in ways:
                    onward(h, 6 - s, i, f, dev)
        return 0

    lax.fori_loop(0, 6, home, 0)
    total = None
    for i in order:
        for f in range(2):
            onward(1, 0, i, f, up_dev)
    for i in order:
        for f in range(2):
            arrive(0, 0, i, f)
            arrive(1, 7, i, f)
        total = co[0, 0, rows(i)] + zr[0, 0, rows(i)].astype(F32) + zr[1, 7, rows(i)].astype(F32)
        if i:
            fs[i - 1] = total.astype(BF16)
            send(fs.at[i - 1], yr.at[i - 1], f_send, f_recv, sub_dev(i))

    ctx_out.wait()
    wait(xb.at[0, 0, 0 : 3 * TOK], y_send)
    wait(xb.at[0, 0:7], ring_send)
    wait(xb.at[1], ring_send)
    wait(pm, mate_send)
    wait(rp, rp_send)
    for u in range(4):
        wait(hr.at[u, 0:7], h_send)
    wait(ym, ym_send)
    wait(zs.at[0, 0:7], z_send)
    wait(zs.at[1], z_send)
    wait(fs, f_send)

    wait(yr, f_recv)
    for n in range(3):
        total = total + yr[n].astype(F32)
    moe_ref[...] = total.astype(BF16)


def keep(v):
    return pltpu.with_memory_space_constraint(v, pltpu.HBM)


def per_device(x_a, routes, route_score, w_gate, w_up, w_down, queries, cache, lengths):
    vmem = pl.BlockSpec(memory_space=pltpu.VMEM)
    hbm = pl.BlockSpec(memory_space=pltpu.HBM)
    dma, dmas = pltpu.SemaphoreType.DMA, lambda *s: pltpu.SemaphoreType.DMA(s)
    return pl.pallas_call(
        kernel,
        out_shape=(
            jax.ShapeDtypeStruct((TOK, WIDTH), BF16),
            jax.ShapeDtypeStruct((1, 128, KV_RANK), BF16),
        ),
        in_specs=[hbm] * 3 + [pl.BlockSpec(memory_space=pltpu.SMEM)] + [hbm] * 5,
        out_specs=(vmem, pl.BlockSpec(memory_space=pl.ANY)),
        scratch_shapes=[
            pltpu.VMEM((8, TOK), jnp.int32),
            pltpu.VMEM((8, TOK), F32),
            pltpu.VMEM((2, 8, 64, WIDE), BF16),
            pltpu.VMEM((WIDTH, FFS), BF16),
            pltpu.VMEM((WIDTH, FFS), BF16),
            pltpu.VMEM((FFS, WIDTH), BF16),
            pltpu.VMEM((576, 128), BF16),
            pltpu.VMEM((576, 128), BF16),
            pltpu.VMEM((128, KV_RANK), BF16),
            pltpu.VMEM((8, 128, 8), F32),
            pltpu.VMEM((8, PAD, WIDTH), BF16),
            pltpu.VMEM((8, PAD, WIDTH), BF16),
            pltpu.VMEM((8, PAD, WIDTH), BF16),
            pltpu.VMEM((8, 4, GROUP, 2 * SHARE), BF16),
            pltpu.VMEM((4, 7, GROUP, 2 * SHARE), BF16),
            pltpu.VMEM((4, 8, GROUP, SHARE), BF16),
            pltpu.VMEM((8, PAD, WIDTH), BF16),
            pltpu.VMEM((8, PAD, WIDTH), BF16),
            pltpu.VMEM((8, PAD, WIDTH), BF16),
            pltpu.VMEM((2, 8, 64, WIDTH), F32),
            pltpu.VMEM((2, 8, 64, WIDTH), BF16),
            pltpu.VMEM((2, 8, 64, WIDTH), BF16),
            pltpu.VMEM((3, TOK, WIDTH), BF16),
            pltpu.VMEM((3, TOK, WIDTH), BF16),
            dmas(9), dma, dmas(4), dma, dmas(2, 8, 4), dma, dmas(8),
            dma, dmas(4), dma, dmas(4, 2), dma, dmas(8), dma, dmas(2, 8, 8), dma, dma,
        ],
        compiler_params=pltpu.CompilerParams(
            collective_id=0, has_side_effects=True, vmem_limit_bytes=48 << 20
        ),
        name="moe_attention",
    )(
        keep(x_a), keep(routes.T), keep(route_score.T), lengths, keep(w_gate), keep(w_up), keep(w_down),
        keep(jnp.swapaxes(queries, 1, 2)), keep(jnp.swapaxes(cache, 1, 2)),
    )


def solution(mesh):
    placed = (
        P(("peer", "sub"), "pool"),
        P(("peer", "sub"), None),
        P(("peer", "sub"), None),
        P("peer", "pool", "sub"),
        P("peer", "pool", "sub"),
        P("peer", "sub", "pool"),
        P(("pool", "peer", "sub"), None, None),
        P(("pool", "peer", "sub"), None, None),
        P(("pool", "peer", "sub")),
    )
    return jax.shard_map(
        per_device,
        mesh=mesh,
        in_specs=placed,
        out_specs=(P(("peer", "sub"), "pool"), P(("pool", "peer", "sub"), None, None)),
        check_vma=False,
    )
```
